128 devices in a mesh: seq: 16 (over y, z), resp: 8 (over x, core).
Axes of the slice: x: 4, y: 4, z: 4, core: 2. Of those that a mesh axis runs over, the one named last changes fastest.
Arguments:
- queries: bfloat16 [64, 32, 8192], P('seq', None, 'resp'), may hold values from -160 to 160
- prompt_keys: bfloat16 [32768, 1024], P('seq', 'resp'), may hold values from -6 to 6
- prompt_values: bfloat16 [32768, 1024], P('seq', 'resp'), may hold values from -6 to 6
- prompt_segment: int32 [32768], P('seq'), may hold values from 0 to 3, never falling along the last dimension, each value on 1 to 16384 neighbouring positions
- own_keys: bfloat16 [64, 2048, 1024], P('seq', None, 'resp'), may hold values from -6 to 6
- own_values: bfloat16 [64, 2048, 1024], P('seq', None, 'resp'), may hold values from -6 to 6
- resp_lengths: int32 [64], P('seq'), may hold values from 1 to 2016, as said below
- resp_groups: int32 [64], P('seq'), may hold values from 0 to 3
- out_weight: bfloat16 [8192, 8192], P('resp', 'seq'), may hold values from -0.0625 to 0.0625
Outputs:
- projected: bfloat16 [64, 32, 8192], P('seq', None, 'resp')
The draws below stay inside these ranges and needn't reach their ends.
Inputs may be any that keep to these rules, and one draw needn't show every extreme that they name: Each response's current tokens sit right after resp_lengths of its own cache positions; the largest value occurs in every draw.
All inputs are finite; a program needn't handle non-finite values.
Results may differ from the reference program's by a relative error of at most 0.015.
Values may be sent and summed in bfloat16 or wider, within the bound.
A program may use at most 576 MiB of HBM per device.

```python
import math
import jax
import jax.numpy as jnp
import numpy as np
from jax import lax

D = 8192
HD = 128
QPK = 8
KV_HEADS = 8
HEADS = 64
R = 64
C = 32
HIST = 2048
PROMPT = 32768
GROUPS = 4


def cache_base(key):
    return jnp.clip(jax.random.normal(key, (R, HIST, KV_HEADS * HD), jnp.float32), -5.0, 5.0)


def draw_own_keys(key, part):
    base = cache_base(key)
    return base.astype(jnp.bfloat16)


def draw_queries(key, part):
    key = jax.random.fold_in(key, 7)
    values = jnp.clip(jax.random.normal(key, (R, C, HEADS * HD), jnp.float32), -5.0, 5.0)
    return values.astype(jnp.bfloat16)


def draw_resp_lengths(key, part):
    key = jax.random.fold_in(key, 9)
    first, second = jax.random.split(key)
    values = jax.random.randint(first, (R,), 1, HIST - C + 1, dtype=jnp.int32)
    order = jax.random.permutation(second, R)
    values = values.at[order[0]].set(HIST - C)
    values = values.at[order[1]].set(1)
    return values


def place_ends(result, rng, least, largest):
    longest = result.shape.index(max(result.shape))
    spots = []
    for shift in (0, 1):
        where = [jax.random.randint(jax.random.fold_in(rng, axis), (), 0, length) for axis, length in enumerate(result.shape)]
        where[longest] = (where[longest] + shift) % result.shape[longest]
        spots.append(tuple(where))
    return result.at[spots[0]].set(least).at[spots[1]].set(largest)


def levels(key, extent, cuts, least, high):
    level, own = 1.0, jax.random.fold_in(key, 6)
    for dim, blocks in cuts:
        heights = jnp.exp(jax.random.uniform(jax.random.fold_in(own, dim), (blocks,), jnp.float32, least / len(cuts), high / len(cuts)))
        level = level * jnp.repeat(heights, extent[dim] // blocks).reshape([-1 if axis == dim else 1 for axis in range(len(extent))])
    return level


def split_up(count, total, reach, skew):
    weights = [(1 << 20) // math.isqrt(rank ** skew) + 1 for rank in range(2, count + 1)]
    spare, holding = total - reach - (count - 1), [1] * (count - 1)
    while spare > 0:
        movable = [i for i in range(count - 1) if holding[i] < reach]
        mass, budget = sum([weights[i] for i in movable]), spare
        for i in movable:
            extra = min(reach - holding[i], max(1, budget * weights[i] // mass), spare)
            holding[i] = holding[i] + extra
            spare = spare - extra
    return np.array([reach] + holding)


def ragged(rng, count, total, bound, slope):
    if count == 2:
        one = jax.random.randint(rng, (), max(1, total - bound), min(bound, total - 1) + 1)
        return jnp.stack([one, total - one])
    lengths = jnp.asarray(split_up(count, total, bound, slope), jnp.int32)
    twos = (count - 1) // 2
    giver, taker = lengths[1:1 + 2 * twos:2], lengths[2:2 + 2 * twos:2]
    margin = jnp.minimum(giver - 1, bound - taker)
    shifted = jax.random.randint(jax.random.fold_in(rng, 1), (twos,), 0, 1 << 20) % (margin + 1)
    lengths = lengths.at[1:1 + 2 * twos:2].set(giver - shifted).at[2:2 + 2 * twos:2].set(taker + shifted)
    return lengths[jax.random.permutation(jax.random.fold_in(rng, 2), count)]


def gaussian(own_key, extent, width, most, pieces=(), kind=jnp.bfloat16):
    entries = jax.random.normal(own_key, extent, jnp.float32) * width
    if len(pieces) > 0:
        entries = levels(own_key, extent, pieces, -0.22, 0.18) * entries
    return jnp.clip(entries, min=-most, max=most).astype(kind)


def setup_inputs(seed: int = 0) -> dict:
    streams_of = jax.random.split(jax.random.key(seed), 10)
    return {
        "queries": draw_queries(jax.random.fold_in(streams_of[9], 71), 0),
        "prompt_keys": gaussian(streams_of[1], (PROMPT, KV_HEADS * HD), 1.0, 6.0, ((0, 16), (1, 8))),
        "prompt_values": gaussian(streams_of[2], (PROMPT, KV_HEADS * HD), 1.0, 6.0, ((0, 16), (1, 8))),
        "prompt_segment": jnp.searchsorted(jnp.cumsum(ragged(streams_of[3], GROUPS, PROMPT, PROMPT // 2, 0)), jnp.arange(PROMPT), side="right").astype(jnp.int32),
        "own_keys": draw_own_keys(jax.random.fold_in(streams_of[9], 71), 0),
        "own_values": gaussian(streams_of[5], (R, HIST, KV_HEADS * HD), 1.0, 6.0, ((0, 16), (2, 8))),
        "resp_lengths": draw_resp_lengths(jax.random.fold_in(streams_of[9], 71), 0),
        "resp_groups": place_ends(jax.random.randint(streams_of[7], (R,), 0, GROUPS), jax.random.fold_in(streams_of[7], 1), 0, GROUPS - 1).astype(jnp.int32),
        "out_weight": gaussian(streams_of[8], (HEADS * HD, D), (HEADS * HD) ** -0.5, 0.0625, ((0, 8), (1, 16))),
    }


NEG = -1e+30

def reference(queries, prompt_keys, prompt_values, prompt_segment, own_keys, own_values, resp_lengths, resp_groups, out_weight):
    factor = 1.0 / math.sqrt(HD)
    key_table = prompt_keys.astype(jnp.float32).reshape(PROMPT, KV_HEADS, HD)
    value_table = prompt_values.astype(jnp.float32).reshape(PROMPT, KV_HEADS, HD)

    def one_response(inputs):
        query_rows, cache_keys, cache_values, length, group = inputs
        query_rows = query_rows.astype(jnp.float32).reshape(C, KV_HEADS, QPK, HD)
        prompt_scores = jnp.einsum('ckqd,pkd->ckqp', query_rows, key_table) * factor
        prompt_allowed = (prompt_segment == group)[None, None, None, :]
        cache_keys = cache_keys.astype(jnp.float32).reshape(HIST, KV_HEADS, HD)
        cache_values = cache_values.astype(jnp.float32).reshape(HIST, KV_HEADS, HD)
        own_scores = jnp.einsum('ckqd,jkd->ckqj', query_rows, cache_keys) * factor
        visible = jnp.arange(HIST, dtype=jnp.int32)[None, :] <= length + jnp.arange(C, dtype=jnp.int32)[:, None]
        own_allowed = visible[:, None, None, :]
        peak = jnp.maximum(lax.optimization_barrier(jnp.max(jnp.where(prompt_allowed, prompt_scores, NEG), axis=-1)), lax.optimization_barrier(jnp.max(jnp.where(own_allowed, own_scores, NEG), axis=-1)))
        prompt_weights = jnp.where(prompt_allowed, jnp.exp(prompt_scores - peak[..., None]), 0.0)
        own_weights = jnp.where(own_allowed, jnp.exp(own_scores - peak[..., None]), 0.0)
        total = lax.optimization_barrier(jnp.sum(prompt_weights, axis=-1)) + lax.optimization_barrier(jnp.sum(own_weights, axis=-1))
        prompt_rounded = lax.optimization_barrier(prompt_weights.astype(jnp.bfloat16)).astype(jnp.float32)
        own_rounded = lax.optimization_barrier(own_weights.astype(jnp.bfloat16)).astype(jnp.float32)
        mixed = jnp.einsum('ckqp,pkd->ckqd', prompt_rounded, value_table)
        mixed = mixed + jnp.einsum('ckqj,jkd->ckqd', own_rounded, cache_values)
        return (mixed / total[..., None]).astype(jnp.bfloat16).reshape(C, HEADS * HD)
    attended = lax.map(one_response, (queries, own_keys, own_values, resp_lengths, resp_groups))
    flat = attended.reshape(R * C, HEADS * HD)
    projected = jnp.dot(flat, out_weight, preferred_element_type=jnp.float32)
    return projected.astype(jnp.bfloat16).reshape(R, C, D)
```

```python
import functools
import math

import jax
import jax.numpy as jnp
from jax import lax
from jax.experimental import pallas as pl
from jax.experimental.pallas import tpu as pltpu
from jax.sharding import PartitionSpec as P

HD = 128
G = 4
SIDE = 4
NEG = -1e30
C2 = math.log2(math.e) / math.sqrt(HD)
ONES = 16
HALF = 512
UNIT = 64
MESH = pl.DeviceIdType.MESH
BF16 = jnp.bfloat16
F32 = jnp.float32


class Place:
    def __init__(self):
        s, r = lax.axis_index("seq"), lax.axis_index("resp")
        self.s, self.r = s, r
        self.at = {"y": s // SIDE, "z": s % SIDE, "x": r // 2, "core": r % 2}

    def step(self, axis, by):
        c = dict(self.at)
        c[axis] = (c[axis] + by + SIDE) % SIDE if axis != "core" else 1 - c[axis]
        return (c["y"] * SIDE + c["z"], c["x"] * 2 + c["core"])

    def index(self, axis, by=0):
        return (self.at[axis] + by + SIDE) % SIDE


AXES = (("z", "y"), ("y", "z"))
BACK, AHEAD = 0, 1


def remote(src, dst, send, recv, to):
    return pltpu.make_async_remote_copy(
        src_ref=src, dst_ref=dst, send_sem=send, recv_sem=recv, device_id=to, device_id_type=MESH
    )


def gather(here, mine, full, near_send, near_recv, far_send, far_recv, hooks=()):
    hooks = list(hooks)
    run = lambda: hooks.pop(0)() if hooks else None
    started = []
    orders = (0, -1, 1, 2)

    def go(copy):
        copy.start()
        started.append(copy)

    def near(X, src, dst, way, kind):
        first, _ = AXES[X]
        to = here.step(first, 1 if way == BACK else -1)
        return remote(src, dst, near_send.at[X, way, kind], near_recv.at[X, way, kind], to)

    def far(X, src, dst, way, kind):
        _, second = AXES[X]
        to = here.step(second, 1 if way == BACK else -1)
        return remote(src, dst, far_send.at[X, way, kind], far_recv.at[X, way, kind], to)

    def slot(X, by2, by1):
        first, second = AXES[X]
        return full[X].at[here.index(second, by2), here.index(first, by1)]

    def along(X, k):
        ref = mine[X] if k == 0 else slot(X, 0, orders[k])
        for way in (BACK, AHEAD):
            go(far(X, ref, slot(X, 0, orders[k]), way, k))

    def landed(X, k, way):
        by2 = -1 if way == BACK else 1
        ref = slot(X, by2, orders[k])
        far(X, ref, ref, way, k).wait_recv()
        if way == (BACK if k < 2 else AHEAD):
            go(far(X, ref, ref, way, 4 + k))

    top, low = pl.ds(0, UNIT), pl.ds(UNIT, UNIT)
    for X in (0, 1):
        for way in (BACK, AHEAD):
            go(near(X, mine[X], slot(X, 0, 0), way, 0))
    for X in (0, 1):
        along(X, 0)
    run()
    for way, by, part in ((BACK, -1, top), (AHEAD, 1, low)):
        for X in (0, 1):
            ref = slot(X, 0, by)
            near(X, ref, ref, way, 0).wait_recv()
            go(near(X, ref.at[part], ref.at[part], way, 1))
            along(X, 1 if way == BACK else 2)
    run()
    for X in (0, 1):
        for way in (BACK, AHEAD):
            landed(X, 0, way)
    for X in (0, 1):
        ref = slot(X, 0, 2)
        near(X, ref.at[top], ref.at[top], BACK, 1).wait_recv()
        near(X, ref.at[low], ref.at[low], AHEAD, 1).wait_recv()
        along(X, 3)
    run()
    for k in (1, 2, 3):
        for X in (0, 1):
            for way in (BACK, AHEAD):
                landed(X, k, way)
        run()
    for k in (0, 1, 2, 3):
        for X in (0, 1):
            ref = slot(X, 2, orders[k])
            far(X, ref, ref, BACK if k < 2 else AHEAD, 4 + k).wait_recv()
    for copy in started:
        copy.wait_send()


def greet(devices, count):
    barrier = pltpu.get_barrier_semaphore()
    for d in devices:
        pl.semaphore_signal(barrier, inc=1, device_id=d, device_id_type=MESH)
    pl.semaphore_wait(barrier, count)


def heads_first(ref, base, rows, heads):
    return jnp.concatenate([ref[pl.ds(base, rows), h * HD : (h + 1) * HD] for h in range(heads)], axis=0)


def transpose_values(v):
    return jnp.transpose(v.astype(F32)).astype(BF16)


def spread_kernel(
    lengths, groups, q, keys, values,
    full0, full1, everyone, own_o, own_st,
    kbuf, vbuf, scores, vt, tile,
    near_send, near_recv, far_send, far_recv, group_send, group_recv, load,
):
    here = Place()
    s, r = here.s, here.r
    n, hist, _ = keys.shape
    C = q.shape[0] // n
    H = q.shape[1] // HD
    rows = C * H
    seqs = SIDE * SIDE
    loads = [pltpu.make_async_copy(keys, kbuf, load.at[0]), pltpu.make_async_copy(values, vbuf, load.at[1])]
    for copy in loads:
        copy.start()
    others = [((s + d) % seqs, r) for d in range(1, seqs)]
    greet(others, seqs - 1)
    lane = lax.broadcasted_iota(jnp.int32, tile.shape, 1)
    mark = jnp.zeros(tile.shape, jnp.int32)
    for i in range(n):
        mark = jnp.where(lane == i, groups[i], mark)
    tile[...] = mark
    told = []
    for d, to in enumerate(others):
        copy = remote(tile, everyone.at[s], group_send.at[d], group_recv.at[d], to)
        copy.start()
        told.append(copy)
    mine = [q.at[:, X * HALF : (X + 1) * HALF] for X in (0, 1)]
    full = (full0, full1)

    def keep():
        for X in (0, 1):
            first, second = AXES[X]
            full[X][here.index(second), here.index(first)] = q[:, X * HALF : (X + 1) * HALF]
        everyone[s] = mark
        own_st[...] = jnp.full(own_st.shape, NEG, F32)
        vt[HD:, :] = jnp.ones((ONES, hist), BF16)
        for copy in loads:
            copy.wait()

    def own(u, _):
        base = pl.multiple_of(u * C, C)
        qa = heads_first(q, base, C, H)
        sc = lax.dot_general(kbuf[u], qa, (((1,), (1,)), ((), ())), preferred_element_type=F32)
        pos = lax.broadcasted_iota(jnp.int32, (hist, rows), 0)
        upto = lengths[u] + lax.broadcasted_iota(jnp.int32, (1, rows), 1) % C
        sc = jnp.where(pos <= upto, sc, NEG)
        scores[...] = sc
        for j in range(0, hist, HD):
            vt[:HD, j : j + HD] = transpose_values(vbuf[u, j : j + HD, :])
        shift = jnp.max(sc, axis=0, keepdims=True) * C2
        p = jnp.exp2(scores[...] * C2 - shift).astype(BF16)
        out = jnp.dot(vt[...], p, preferred_element_type=F32)
        total = out[HD : HD + 1, :]
        lse = shift + jnp.log2(total)
        out = out[:HD, :] * (1.0 / total)
        for X in (0, 1):
            own_st[X, u // 2, pl.ds(u % 2, 1), :] = lse[:, X * HD : (X + 1) * HD]
            t = jnp.transpose(out[:, X * HD : (X + 1) * HD])
            for w in range(HD // C):
                own_o[X, u // 2, pl.ds(pl.multiple_of(u % 2 * C, C), C), w * HD : (w + 1) * HD] = t[w * C : (w + 1) * C, :]
        return 0

    gather(
        here, mine, full, near_send, near_recv, far_send, far_recv,
        hooks=(keep, lambda: lax.fori_loop(0, n, own, 0)),
    )
    for d, copy in enumerate(told):
        copy.wait_send()
        src = everyone.at[(s + seqs - 1 - d) % seqs]
        remote(src, src, group_send.at[d], group_recv.at[d], others[d]).wait_recv()


def spread(lengths, groups, q, keys, values):
    n, hist, _ = keys.shape
    C = q.shape[0] // n
    rows = C * q.shape[1] // HD
    vm, sm, hbm = (pl.BlockSpec(memory_space=m) for m in (pltpu.VMEM, pltpu.SMEM, pl.ANY))
    dma = pltpu.SemaphoreType.DMA
    full = jax.ShapeDtypeStruct((SIDE, SIDE, n * C, HALF), BF16)
    return pl.pallas_call(
        spread_kernel,
        out_shape=(
            full,
            full,
            jax.ShapeDtypeStruct((SIDE * SIDE, 8, HD), jnp.int32),
            jax.ShapeDtypeStruct((2, 2, UNIT, HALF), F32),
            jax.ShapeDtypeStruct((2, 2, 8, HD), F32),
        ),
        in_specs=[sm, sm, vm, hbm, hbm],
        out_specs=(vm,) * 5,
        scratch_shapes=[
            pltpu.VMEM(keys.shape, BF16),
            pltpu.VMEM(keys.shape, BF16),
            pltpu.VMEM((hist, rows), F32),
            pltpu.VMEM((HD + ONES, hist), BF16),
            pltpu.VMEM((8, HD), jnp.int32),
            dma((2, 2, 2)), dma((2, 2, 2)), dma((2, 2, 8)), dma((2, 2, 8)),
            dma((SIDE * SIDE - 1,)), dma((SIDE * SIDE - 1,)), dma((2,)),
        ],
        compiler_params=pltpu.CompilerParams(collective_id=1, has_side_effects=True, vmem_limit_bytes=50 << 20),
        name="spread_queries",
    )(lengths, groups, q, keys, values)


def prompt_kernel(sizes, groups, seg, q0, q1, k, v, o0, o1, st0, st1, lists, count, sa, sb, vt, ka):
    n_resp = groups.shape[0]
    C = q0.shape[0] // n_resp
    H = 2 * HALF // HD
    L = k.shape[0]
    rows = C * H
    per = 4
    for ref in (st0, st1):
        ref[...] = jnp.full(ref.shape, NEG, F32)
    for ref in (o0, o1):
        ref[...] = jnp.zeros(ref.shape, BF16)
    for j in range(0, L, HD):
        vt[:HD, j : j + HD] = transpose_values(v[j : j + HD, :])
    vt[HD:, :] = jnp.ones((ONES, L), BF16)
    sg = seg[...]
    cut = [jnp.int32(0)] + [jnp.sum((sg < g).astype(jnp.int32)) for g in range(1, G)] + [jnp.int32(L)]
    lane = lax.broadcasted_iota(jnp.int32, (1, HD), 1)
    low, high = jnp.zeros((1, HD), jnp.int32), jnp.full((1, HD), L, jnp.int32)
    for g in range(G):
        low = jnp.where(lane == g, cut[g], low)
        high = jnp.where(lane == g, cut[g + 1], high)
        count[g] = 0
    ka[:, :HD] = k[...]
    pos = lax.broadcasted_iota(jnp.int32, (L, HD), 0)
    ka[:, HD:] = jnp.where(jnp.logical_and(pos >= low, pos < high), 0.0, NEG).astype(BF16)

    def scan(r, _):
        g = groups[r]
        c = count[g]
        lists[g * n_resp + c] = r
        count[g] = c + 1
        return 0

    lax.fori_loop(0, n_resp, scan, 0)

    def spots(r):
        s, u = r // per, r % per
        turned = (s % SIDE) * SIDE + s // SIDE
        return s, turned, u

    def score(g, n, i, p0, T, dst):
        s, turned, u = spots(lists[g * n_resp + jnp.minimum(i, n - 1)])
        base0 = pl.multiple_of((s * per + u) * C, C)
        base1 = pl.multiple_of((turned * per + u) * C, C)
        mine = jnp.concatenate([heads_first(q0, base0, C, H // 2), heads_first(q1, base1, C, H // 2)], axis=0)
        flag = (lax.broadcasted_iota(jnp.int32, (rows, HD), 1) == g).astype(F32).astype(BF16)
        qa = jnp.concatenate([mine, flag], axis=1)
        sc = lax.dot_general(ka[pl.ds(p0, T), :], qa, (((1,), (1,)), ((), ())), preferred_element_type=F32)
        dst[:T, :] = sc
        return jnp.max(sc, axis=0, keepdims=True)

    def soft(g, n, i, p0, T, src, top):
        s, turned, u = spots(lists[g * n_resp + jnp.minimum(i, n - 1)])
        shift = top * C2
        p = jnp.exp2(src[:T, :] * C2 - shift).astype(BF16)
        out = jnp.dot(vt[:, pl.ds(p0, T)], p, preferred_element_type=F32)
        total = out[HD : HD + 1, :]
        lse = shift + jnp.log2(total)
        out = out[:HD, :] * (1.0 / total)
        for X, o, st, place in ((0, o0, st0, turned), (1, o1, st1, s)):
            st[pl.ds((place * 2 + u // 2) * 8 + u % 2, 1), :] = lse[:, X * HD : (X + 1) * HD]
            base = pl.multiple_of((place * per + u) * C, C)
            t = jnp.transpose(out[:, X * HD : (X + 1) * HD]).astype(BF16)
            for w in range(HD // C):
                o[pl.ds(base, C), w * HD : (w + 1) * HD] = t[w * C : (w + 1) * C, :]

    for g in range(G):
        lo, hi, n = cut[g], cut[g + 1], count[g]
        start = lo // HD * HD
        for T, less in zip(sizes, (0,) + sizes[:-1]):
            p0 = pl.multiple_of(jnp.minimum(start, L - T), HD)
            fits = hi - p0 <= T
            if less:
                fits = jnp.logical_and(fits, hi - jnp.minimum(start, L - less) > less)

            @pl.when(jnp.logical_and(jnp.logical_and(hi > lo, n > 0), fits))
            def _(T=T, p0=p0, n=n, g=g):
                def two(i, top):
                    j = 2 * i
                    after = score(g, n, j + 1, p0, T, sb)
                    soft(g, n, j, p0, T, sa, top)
                    then = score(g, n, j + 2, p0, T, sa)
                    soft(g, n, j + 1, p0, T, sb, after)
                    return then

                lax.fori_loop(0, (n + 1) // 2, two, score(g, n, 0, p0, T, sa))


def prompt_part(groups, seg, q0, q1, k, v):
    L = k.shape[0]
    rows, width = q0.shape
    R = rows // groups.shape[0] * 2 * width // HD
    vm = pl.BlockSpec(memory_space=pltpu.VMEM)
    part = jax.ShapeDtypeStruct(q0.shape, BF16)
    stat = jax.ShapeDtypeStruct((rows // UNIT * 8, HD), F32)
    sizes = tuple(L * i // 4 for i in (1, 2, 3, 4))
    return pl.pallas_call(
        functools.partial(prompt_kernel, sizes),
        out_shape=(part, part, stat, stat),
        in_specs=[pl.BlockSpec(memory_space=pltpu.SMEM)] + [vm] * 5,
        out_specs=(vm,) * 4,
        scratch_shapes=[
            pltpu.SMEM((G * groups.shape[0],), jnp.int32),
            pltpu.SMEM((G,), jnp.int32),
            pltpu.VMEM((L, R), F32),
            pltpu.VMEM((L, R), F32),
            pltpu.VMEM((HD + ONES, L), BF16),
            pltpu.VMEM((L, 2 * HD), BF16),
        ],
        compiler_params=pltpu.CompilerParams(vmem_limit_bytes=50 << 20),
        name="prompt_part",
    )(groups, seg.reshape(-1, HD), q0, q1, k, v)


def merge(parts):
    top = functools.reduce(jnp.maximum, [st for _, st in parts])
    weights = [jnp.exp2(st - top) for _, st in parts]
    total = functools.reduce(jnp.add, weights)
    scale = 1.0 / total
    turned = [jnp.transpose(w * scale) for w in weights]
    C = UNIT // 2
    lines = []
    for u in range(2):
        line = []
        for h in range(HALF // HD):
            acc = None
            for (o, _), t in zip(parts, turned):
                term = o[u * C : (u + 1) * C, h * HD : (h + 1) * HD].astype(F32) * t[h * C : (h + 1) * C, u : u + 1]
                acc = term if acc is None else acc + term
            line.append(acc)
        lines.append(jnp.concatenate(line, axis=1))
    return jnp.concatenate(lines, axis=0).astype(BF16), top + jnp.log2(total)


class Ring:
    def __init__(self, here, axis, src, in2, in1, out, sems, units):
        self.here, self.axis, self.src, self.in2, self.in1, self.out = here, axis, src, in2, in1, out
        self.send, self.recv = sems
        self.units, self.half = units, units // 2
        self.started = []

    def copy(self, src, dst, way, kind):
        to = self.here.step(self.axis, 1 if way == BACK else -1)
        return [
            remote(a, b, self.send.at[way, kind, i], self.recv.at[way, kind, i], to)
            for i, (a, b) in enumerate(zip(src, dst))
        ]

    def go(self, copies):
        for c in copies:
            c.start()
            self.started.append(c)

    def line(self, by, lo, count):
        i = self.here.index(self.axis, by)
        return [ref.at[i, pl.ds(lo, count)] for ref in self.src]

    def part(self, refs, way, lo, count):
        return [ref.at[way, pl.ds(lo, count)] for ref in refs]

    def begin_far(self):
        h = self.half
        self.go(self.copy(self.line(2, 0, h), self.part(self.in2, BACK, 0, h), BACK, 0))
        self.go(self.copy(self.line(2, h, h), self.part(self.in2, AHEAD, 0, h), AHEAD, 0))

    def begin_near(self):
        h = self.half
        self.go(self.copy(self.line(1, h, h), self.part(self.in1, BACK, h, h), BACK, 1))
        self.go(self.copy(self.line(-1, 0, h), self.part(self.in1, AHEAD, 0, h), AHEAD, 1))

    def pass_on(self, way):
        h = self.half
        lo, by = (0, 1) if way == BACK else (h, -1)
        got = self.part(self.in2, way, 0, h)
        for c in self.copy(got, got, way, 0):
            c.wait_recv()
        i = self.here.index(self.axis, by)

        def one(u, _):
            mine = [ref[i, lo + u] for ref in self.src]
            theirs = [ref[way, u] for ref in self.in2]
            for ref, value in zip(self.out, self.join([mine, theirs])):
                ref[way, u] = value
            return 0

        lax.fori_loop(0, h, one, 0)
        self.go(self.copy(self.part(self.out, way, 0, h), self.part(self.in1, way, lo, h), way, 2))

    def arrive(self):
        h = self.half
        for way, raw, sent in ((BACK, h, 0), (AHEAD, 0, h)):
            for kind, lo in ((1, raw), (2, sent)):
                got = self.part(self.in1, way, lo, h)
                for c in self.copy(got, got, way, kind):
                    c.wait_recv()

    def total(self, u, extra=()):
        i = self.here.index(self.axis)
        parts = [[ref[i, u] for ref in self.src]] + [[ref[way, u] for ref in self.in1] for way in (BACK, AHEAD)]
        return self.join(parts + list(extra))

    def join(self, parts):
        return merge(parts)

    def finish(self):
        for c in self.started:
            c.wait_send()


class PlainRing(Ring):
    def join(self, parts):
        return [functools.reduce(jnp.add, [p[0].astype(F32) for p in parts]).astype(BF16)]


def project_kernel(
    o0, o1, st0, st1, own_o, own_st, weight, result,
    a_in2, a_in2s, a_in1, a_in1s, a_out, a_outs, a_sum, a_sums,
    b_in2, b_in2s, b_in1, b_in1s, b_out, b_outs,
    att, full0, full1, part, swapped, sums, x_in2, x_in1, x_out, final,
    a_send, a_recv, b_send, b_recv, x_send, x_recv,
    near_send, near_recv, far_send, far_recv, core_send, core_recv, last_send, last_recv, local,
):
    here = Place()
    s, r = here.s, here.r
    x, core = here.at["x"], here.at["core"]
    seqs, resps = SIDE * SIDE, 2 * SIDE
    to = [(2 * r + i, s // 2) for i in range(2)]
    source = [(2 * r + i, s // 2) for i in range(2)]
    stays = s // 2 == r
    mate = here.step("core", 1)
    near = [here.step(axis, by) for axis in ("y", "z", "x") for by in (1, -1)] + [mate]
    barrier = pltpu.get_barrier_semaphore()
    for d in near:
        pl.semaphore_signal(barrier, inc=1, device_id=d, device_id_type=MESH)
    for i in range(2):

        @pl.when(jnp.logical_not(jnp.logical_and(stays, s % 2 == i)))
        def _():
            pl.semaphore_signal(barrier, inc=1, device_id=to[i], device_id_type=MESH)

    pl.semaphore_wait(barrier, len(near) + 2 - stays.astype(jnp.int32))

    o, st = (o0, o1), (st0, st1)
    one = [
        Ring(
            here, AXES[X][0], (o[X], st[X]), (a_in2.at[X], a_in2s.at[X]), (a_in1.at[X], a_in1s.at[X]),
            (a_out.at[X], a_outs.at[X]), (a_send.at[X], a_recv.at[X]), 2 * SIDE,
        )
        for X in (0, 1)
    ]
    two = [
        Ring(
            here, AXES[X][1], (a_sum.at[X], a_sums.at[X]), (b_in2.at[X], b_in2s.at[X]), (b_in1.at[X], b_in1s.at[X]),
            (b_out.at[X], b_outs.at[X]), (b_send.at[X], b_recv.at[X]), 2,
        )
        for X in (0, 1)
    ]
    for X in (0, 1):
        one[X].begin_far()
    for X in (0, 1):
        one[X].begin_near()
    for way in (BACK, AHEAD):
        for X in (0, 1):
            one[X].pass_on(way)
    for X in (0, 1):
        one[X].arrive()

    def settle(by):
        for X in (0, 1):
            d = here.index(AXES[X][1], by)

            def each(u, _, X=X, d=d):
                value, stat = one[X].total(2 * d + u)
                a_sum[X, d, u] = value
                a_sums[X, d, u] = stat
                return 0

            lax.fori_loop(0, 2, each, 0)

    settle(2)
    for X in (0, 1):
        two[X].begin_far()
    settle(1)
    settle(-1)
    for X in (0, 1):
        two[X].begin_near()
    for way in (BACK, AHEAD):
        for X in (0, 1):
            two[X].pass_on(way)
    settle(0)
    for X in (0, 1):
        two[X].arrive()
        for u in range(2):
            value, _ = two[X].total(u, [(own_o[X, u], own_st[X, u])])
            att[X, u * UNIT : (u + 1) * UNIT, :] = value
    for X in (0, 1):
        one[X].finish()
        two[X].finish()

    full = (full0, full1)

    def keep():
        for X in (0, 1):
            first, second = AXES[X]
            full[X][here.index(second), here.index(first)] = att[X]

    gather(here, (att.at[0], att.at[1]), full, near_send, near_recv, far_send, far_recv, hooks=(keep,))

    def term(line, c):
        for i in range(2):
            owner = (line * 2 + c) * 2 + i
            y, z = owner // SIDE, owner % SIDE
            value = jnp.dot(full0[y, z], weight[:HALF, :], preferred_element_type=F32)
            value += jnp.dot(full1[z, y], weight[HALF:, :], preferred_element_type=F32)
            part[line, c, i] = value.astype(BF16)

    crossing = []
    lines = [here.index("x", by) for by in (2, 1, -1, 0)]
    ring = PlainRing(here, "x", (sums,), (x_in2,), (x_in1,), (x_out,), (x_send, x_recv), 2)

    def work(k):
        line = lines[k]
        term(line, 1 - core)
        copy = remote(part.at[line, 1 - core], swapped.at[line], core_send.at[k], core_recv.at[k], mate)
        copy.start()
        crossing.append(copy)
        term(line, core)

    def add(k):
        line = lines[k]
        crossing[k].wait_recv()
        sums[line] = (part[line, core].astype(F32) + swapped[line].astype(F32)).astype(BF16)

    work(0)
    work(1)
    add(0)
    ring.begin_far()
    work(2)
    add(1)
    add(2)
    ring.begin_near()
    work(3)
    for way in (BACK, AHEAD):
        ring.pass_on(way)
    add(3)
    ring.arrive()
    for copy in crossing:
        copy.wait_send()

    for i in range(2):
        final[i] = ring.total(i)[0]
        mine = jnp.logical_and(stays, s % 2 == i)
        columns = pl.ds(pl.multiple_of(s % 2 * HALF, HALF), HALF)

        @pl.when(jnp.logical_not(mine))
        def _():
            remote(final.at[i], result.at[:, columns], last_send.at[i], last_recv.at[s % 2], to[i]).start()

        @pl.when(mine)
        def _():
            pltpu.make_async_copy(final.at[i], result.at[:, columns], local).start()

    ring.finish()
    for i in range(2):
        mine = jnp.logical_and(stays, s % 2 == i)
        columns = pl.ds(i * HALF, HALF)

        @pl.when(jnp.logical_not(mine))
        def _():
            copy = remote(final.at[i], result.at[:, columns], last_send.at[i], last_recv.at[i], source[i])
            copy.wait_send()
            copy.wait_recv()

        @pl.when(mine)
        def _():
            pltpu.make_async_copy(final.at[i], result.at[:, columns], local).wait()


def project(o0, o1, st0, st1, own_o, own_st, weight):
    vm = pl.BlockSpec(memory_space=pltpu.VMEM)
    dma = pltpu.SemaphoreType.DMA
    block, stat = (UNIT, HALF), (8, HD)
    rows = 2 * UNIT
    o0, o1 = (a.reshape(SIDE, 2 * SIDE, *block) for a in (o0, o1))
    st0, st1 = (a.reshape(SIDE, 2 * SIDE, *stat) for a in (st0, st1))
    pair = lambda *lead: [pltpu.VMEM(lead + block, BF16), pltpu.VMEM(lead + stat, F32)]
    return pl.pallas_call(
        project_kernel,
        out_shape=jax.ShapeDtypeStruct((rows, 2 * HALF), BF16),
        in_specs=[vm] * 7,
        out_specs=vm,
        scratch_shapes=[
            *pair(2, 2, SIDE), *pair(2, 2, 2 * SIDE), *pair(2, 2, SIDE), *pair(2, SIDE, 2),
            *pair(2, 2, 1), *pair(2, 2, 2), *pair(2, 2, 1),
            pltpu.VMEM((2, rows, HALF), BF16),
            pltpu.VMEM((SIDE, SIDE, rows, HALF), BF16),
            pltpu.VMEM((SIDE, SIDE, rows, HALF), BF16),
            pltpu.VMEM((SIDE, 2, 2, rows, HALF), BF16),
            pltpu.VMEM((SIDE, 2, rows, HALF), BF16),
            pltpu.VMEM((SIDE, 2, rows, HALF), BF16),
            pltpu.VMEM((2, 1, rows, HALF), BF16),
            pltpu.VMEM((2, 2, rows, HALF), BF16),
            pltpu.VMEM((2, 1, rows, HALF), BF16),
            pltpu.VMEM((2, rows, HALF), BF16),
            dma((2, 2, 3, 2)), dma((2, 2, 3, 2)), dma((2, 2, 3, 2)), dma((2, 2, 3, 2)),
            dma((2, 3, 1)), dma((2, 3, 1)),
            dma((2, 2, 2)), dma((2, 2, 2)), dma((2, 2, 8)), dma((2, 2, 8)),
            dma((SIDE,)), dma((SIDE,)), dma((2,)), dma((2,)), dma,
        ],
        compiler_params=pltpu.CompilerParams(collective_id=2, has_side_effects=True, vmem_limit_bytes=56 << 20),
        name="merge_and_project",
    )(o0, o1, st0, st1, own_o, own_st, weight)


def per_device(
    queries, prompt_keys, prompt_values, prompt_segment, own_keys, own_values, resp_lengths, resp_groups, out_weight
):
    n, C, width = queries.shape
    q = queries.reshape(n * C, width)
    full0, full1, everyone, own_o, own_st = spread(resp_lengths, resp_groups, q, own_keys, own_values)
    groups = everyone[:, 0, :n].reshape(-1)
    flat = lambda a: a.reshape(-1, HALF)
    parts = prompt_part(groups, prompt_segment, flat(full0), flat(full1), prompt_keys, prompt_values)
    return project(*parts, own_o, own_st, out_weight).reshape(n, C, width)


def solution(mesh):
    in_specs = (
        P("seq", None, "resp"),
        P("seq", "resp"),
        P("seq", "resp"),
        P("seq"),
        P("seq", None, "resp"),
        P("seq", None, "resp"),
        P("seq"),
        P("seq"),
        P("resp", "seq"),
    )
    return jax.shard_map(
        per_device, mesh=mesh, in_specs=in_specs, out_specs=P("seq", None, "resp"), check_vma=False
    )
```

```python
import functools
import math

import jax
import jax.numpy as jnp
from jax import lax
from jax.experimental import pallas as pl
from jax.experimental.pallas import tpu as pltpu
from jax.sharding import PartitionSpec as P

HD = 128
G = 4
SIDE = 4
NEG = -1e30
C2 = math.log2(math.e) / math.sqrt(HD)
ONES = 16
HALF = 512
UNIT = 64
MESH = pl.DeviceIdType.MESH
BF16 = jnp.bfloat16
F32 = jnp.float32


class Place:
    def __init__(self):
        s, r = lax.axis_index("seq"), lax.axis_index("resp")
        self.s, self.r = s, r
        self.at = {"y": s // SIDE, "z": s % SIDE, "x": r // 2, "core": r % 2}

    def step(self, axis, by):
        c = dict(self.at)
        c[axis] = (c[axis] + by + SIDE) % SIDE if axis != "core" else 1 - c[axis]
        return (c["y"] * SIDE + c["z"], c["x"] * 2 + c["core"])

    def index(self, axis, by=0):
        return (self.at[axis] + by + SIDE) % SIDE


AXES = (("z", "y"), ("y", "z"))
BACK, AHEAD = 0, 1


def remote(src, dst, send, recv, to):
    return pltpu.make_async_remote_copy(
        src_ref=src, dst_ref=dst, send_sem=send, recv_sem=recv, device_id=to, device_id_type=MESH
    )


def gather(here, mine, full, near_send, near_recv, far_send, far_recv):
    started = []
    orders = (0, -1, 1, 2)

    def go(copy):
        copy.start()
        started.append(copy)

    def near(X, src, dst, way, kind):
        to = here.step(AXES[X][0], 1 if way == BACK else -1)
        return remote(src, dst, near_send.at[X, way, kind], near_recv.at[X, way, kind], to)

    def far(X, src, dst, way, kind):
        to = here.step(AXES[X][1], 1 if way == BACK else -1)
        return remote(src, dst, far_send.at[X, way, kind], far_recv.at[X, way, kind], to)

    def slot(X, by2, by1):
        first, second = AXES[X]
        return full[X].at[here.index(second, by2), here.index(first, by1)]

    def along(X, k):
        ref = mine[X] if k == 0 else slot(X, 0, orders[k])
        for way in (BACK, AHEAD):
            go(far(X, ref, slot(X, 0, orders[k]), way, k))

    def landed(k):
        for X in (0, 1):
            for way in (BACK, AHEAD):
                ref = slot(X, -1 if way == BACK else 1, orders[k])
                far(X, ref, ref, way, k).wait_recv()
                if way == (BACK if k < 2 else AHEAD):
                    go(far(X, ref, ref, way, 4 + k))

    top, low = pl.ds(0, UNIT), pl.ds(UNIT, UNIT)
    for X in (0, 1):
        for way in (BACK, AHEAD):
            go(near(X, mine[X], slot(X, 0, 0), way, 0))
    for X in (0, 1):
        along(X, 0)
    yield "sent"
    for way, by, part in ((BACK, -1, top), (AHEAD, 1, low)):
        for X in (0, 1):
            ref = slot(X, 0, by)
            near(X, ref, ref, way, 0).wait_recv()
            go(near(X, ref.at[part], ref.at[part], way, 1))
            along(X, 1 if way == BACK else 2)
    yield "near"
    landed(0)
    yield "far0"
    for X in (0, 1):
        ref = slot(X, 0, 2)
        near(X, ref.at[top], ref.at[top], BACK, 1).wait_recv()
        near(X, ref.at[low], ref.at[low], AHEAD, 1).wait_recv()
        along(X, 3)
    yield "line"
    for k in (1, 2, 3):
        landed(k)
        yield "far" + str(k)
    for k in (0, 1, 2, 3):
        for X in (0, 1):
            ref = slot(X, 2, orders[k])
            far(X, ref, ref, BACK if k < 2 else AHEAD, 4 + k).wait_recv()
        yield "past" + str(k)
    for copy in started:
        copy.wait_send()


def greet(devices, count):
    barrier = pltpu.get_barrier_semaphore()
    for d in devices:
        pl.semaphore_signal(barrier, inc=1, device_id=d, device_id_type=MESH)
    pl.semaphore_wait(barrier, count)


def heads_first(ref, base, rows, heads):
    return jnp.concatenate([ref[pl.ds(base, rows), h * HD : (h + 1) * HD] for h in range(heads)], axis=0)


def transpose_values(v):
    return jnp.transpose(v.astype(F32)).astype(BF16)


def spread_kernel(
    lengths, groups, q, keys, values,
    full0, full1, everyone, own_o, own_st,
    qbuf, kbuf, vbuf, lens, marks, scores, vt, tile,
    near_send, near_recv, far_send, far_recv, group_send, group_recv, load,
):
    here = Place()
    s, r = here.s, here.r
    n, hist, _ = keys.shape
    C = q.shape[0] // n
    H = q.shape[1] // HD
    rows = C * H
    seqs = SIDE * SIDE
    loads = [
        pltpu.make_async_copy(src, dst, load.at[i])
        for i, (src, dst) in enumerate(((groups, marks), (lengths, lens), (q, qbuf), (keys, kbuf), (values, vbuf)))
    ]
    for copy in loads:
        copy.start()
    others = [((s + d) % seqs, r) for d in range(1, seqs)]
    greet(others, seqs - 1)
    mine = [q.at[:, X * HALF : (X + 1) * HALF] for X in (0, 1)]
    full = (full0, full1)
    steps = gather(here, mine, full, near_send, near_recv, far_send, far_recv)
    next(steps)
    loads[0].wait()
    lane = lax.broadcasted_iota(jnp.int32, tile.shape, 1)
    mark = jnp.zeros(tile.shape, jnp.int32)
    for i in range(n):
        mark = jnp.where(lane == i, marks[i], mark)
    tile[...] = mark
    told = []
    for d, to in enumerate(others):
        copy = remote(tile, everyone.at[s], group_send.at[d], group_recv.at[d], to)
        copy.start()
        told.append(copy)
    for copy in loads[1:]:
        copy.wait()
    for X in (0, 1):
        first, second = AXES[X]
        full[X][here.index(second), here.index(first)] = qbuf[:, X * HALF : (X + 1) * HALF]
    everyone[s] = mark
    own_st[...] = jnp.full(own_st.shape, NEG, F32)
    vt[HD:, :] = jnp.ones((ONES, hist), BF16)

    def own(u, _):
        base = pl.multiple_of(u * C, C)
        qa = heads_first(qbuf, base, C, H)
        sc = lax.dot_general(kbuf[u], qa, (((1,), (1,)), ((), ())), preferred_element_type=F32)
        pos = lax.broadcasted_iota(jnp.int32, (hist, rows), 0)
        upto = lens[u] + lax.broadcasted_iota(jnp.int32, (1, rows), 1) % C
        sc = jnp.where(pos <= upto, sc, NEG)
        scores[...] = sc
        for j in range(0, hist, HD):
            vt[:HD, j : j + HD] = transpose_values(vbuf[u, j : j + HD, :])
        shift = jnp.max(sc, axis=0, keepdims=True) * C2
        p = jnp.exp2(scores[...] * C2 - shift).astype(BF16)
        out = jnp.dot(vt[...], p, preferred_element_type=F32)
        total = out[HD : HD + 1, :]
        lse = shift + jnp.log2(total)
        out = out[:HD, :] * (1.0 / total)
        for X in (0, 1):
            own_st[X, u // 2, pl.ds(u % 2, 1), :] = lse[:, X * HD : (X + 1) * HD]
            t = jnp.transpose(out[:, X * HD : (X + 1) * HD])
            for w in range(HD // C):
                own_o[X, u // 2, pl.ds(pl.multiple_of(u % 2 * C, C), C), w * HD : (w + 1) * HD] = t[w * C : (w + 1) * C, :]
        return 0

    lax.fori_loop(0, n // 2, own, 0)
    for stage in steps:
        if stage == "far0":
            lax.fori_loop(n // 2, n, own, 0)
    for d, copy in enumerate(told):
        copy.wait_send()
        src = everyone.at[(s + seqs - 1 - d) % seqs]
        remote(src, src, group_send.at[d], group_recv.at[d], others[d]).wait_recv()


def spread(lengths, groups, q, keys, values):
    n, hist, _ = keys.shape
    C = q.shape[0] // n
    rows = C * q.shape[1] // HD
    vm, hbm = (pl.BlockSpec(memory_space=m) for m in (pltpu.VMEM, pltpu.HBM))
    dma = pltpu.SemaphoreType.DMA
    full = jax.ShapeDtypeStruct((SIDE, SIDE, n * C, HALF), BF16)
    return pl.pallas_call(
        spread_kernel,
        out_shape=(
            full,
            full,
            jax.ShapeDtypeStruct((SIDE * SIDE, 8, HD), jnp.int32),
            jax.ShapeDtypeStruct((2, 2, UNIT, HALF), F32),
            jax.ShapeDtypeStruct((2, 2, 8, HD), F32),
        ),
        in_specs=[hbm] * 5,
        out_specs=(vm,) * 5,
        scratch_shapes=[
            pltpu.VMEM(q.shape, BF16),
            pltpu.VMEM(keys.shape, BF16),
            pltpu.VMEM(keys.shape, BF16),
            pltpu.SMEM((n,), jnp.int32),
            pltpu.SMEM((n,), jnp.int32),
            pltpu.VMEM((hist, rows), F32),
            pltpu.VMEM((HD + ONES, hist), BF16),
            pltpu.VMEM((8, HD), jnp.int32),
            dma((2, 2, 2)), dma((2, 2, 2)), dma((2, 2, 8)), dma((2, 2, 8)),
            dma((SIDE * SIDE - 1,)), dma((SIDE * SIDE - 1,)), dma((5,)),
        ],
        compiler_params=pltpu.CompilerParams(collective_id=1, has_side_effects=True, vmem_limit_bytes=24 << 20),
        name="spread_queries",
    )(*(pltpu.with_memory_space_constraint(a, pltpu.HBM) for a in (lengths, groups, q, keys, values)))


def prompt_kernel(sizes, everyone, seg, q0, q1, k, v, o0, o1, st0, st1, lists, count, sa, sb, vt, ka, groups, load):
    fetch = pltpu.make_async_copy(everyone.at[:, 0:1], groups, load)
    fetch.start()
    n_resp = everyone.shape[0] * 4
    C = q0.shape[0] // n_resp
    H = 2 * HALF // HD
    L = k.shape[0]
    rows = C * H
    per = 4
    for ref in (st0, st1):
        ref[...] = jnp.full(ref.shape, NEG, F32)
    for ref in (o0, o1):
        ref[...] = jnp.zeros(ref.shape, BF16)
    for j in range(0, L, HD):
        vt[:HD, j : j + HD] = transpose_values(v[j : j + HD, :])
    vt[HD:, :] = jnp.ones((ONES, L), BF16)
    sg = seg[...]
    cut = [jnp.int32(0)] + [jnp.sum((sg < g).astype(jnp.int32)) for g in range(1, G)] + [jnp.int32(L)]
    lane = lax.broadcasted_iota(jnp.int32, (1, HD), 1)
    low, high = jnp.zeros((1, HD), jnp.int32), jnp.full((1, HD), L, jnp.int32)
    for g in range(G):
        low = jnp.where(lane == g, cut[g], low)
        high = jnp.where(lane == g, cut[g + 1], high)
        count[g] = 0
    ka[:, :HD] = k[...]
    pos = lax.broadcasted_iota(jnp.int32, (L, HD), 0)
    ka[:, HD:] = jnp.where(jnp.logical_and(pos >= low, pos < high), 0.0, NEG).astype(BF16)

    def scan(r, _):
        g = groups[r // per, 0, r % per]
        c = count[g]
        lists[g * n_resp + c] = r
        count[g] = c + 1
        return 0

    fetch.wait()
    lax.fori_loop(0, n_resp, scan, 0)

    def spots(r):
        s, u = r // per, r % per
        turned = (s % SIDE) * SIDE + s // SIDE
        return s, turned, u

    def score(g, n, i, p0, T, dst):
        s, turned, u = spots(lists[g * n_resp + jnp.minimum(i, n - 1)])
        base0 = pl.multiple_of((s * per + u) * C, C)
        base1 = pl.multiple_of((turned * per + u) * C, C)
        mine = jnp.concatenate([heads_first(q0, base0, C, H // 2), heads_first(q1, base1, C, H // 2)], axis=0)
        flag = (lax.broadcasted_iota(jnp.int32, (rows, HD), 1) == g).astype(F32).astype(BF16)
        qa = jnp.concatenate([mine, flag], axis=1)
        sc = lax.dot_general(ka[pl.ds(p0, T), :], qa, (((1,), (1,)), ((), ())), preferred_element_type=F32)
        dst[:T, :] = sc
        return jnp.max(sc, axis=0, keepdims=True)

    def soft(g, n, i, p0, T, src, top):
        s, turned, u = spots(lists[g * n_resp + jnp.minimum(i, n - 1)])
        shift = top * C2
        p = jnp.exp2(src[:T, :] * C2 - shift).astype(BF16)
        out = jnp.dot(vt[:, pl.ds(p0, T)], p, preferred_element_type=F32)
        total = out[HD : HD + 1, :]
        lse = shift + jnp.log2(total)
        out = out[:HD, :] * (1.0 / total)
        for X, o, st, place in ((0, o0, st0, turned), (1, o1, st1, s)):
            st[pl.ds((place * 2 + u // 2) * 8 + u % 2, 1), :] = lse[:, X * HD : (X + 1) * HD]
            base = pl.multiple_of((place * per + u) * C, C)
            t = jnp.transpose(out[:, X * HD : (X + 1) * HD]).astype(BF16)
            for w in range(HD // C):
                o[pl.ds(base, C), w * HD : (w + 1) * HD] = t[w * C : (w + 1) * C, :]

    for g in range(G):
        lo, hi, n = cut[g], cut[g + 1], count[g]
        start = lo // HD * HD
        for T, less in zip(sizes, (0,) + sizes[:-1]):
            p0 = pl.multiple_of(jnp.minimum(start, L - T), HD)
            fits = hi - p0 <= T
            if less:
                fits = jnp.logical_and(fits, hi - jnp.minimum(start, L - less) > less)

            @pl.when(jnp.logical_and(jnp.logical_and(hi > lo, n > 0), fits))
            def _(T=T, p0=p0, n=n, g=g):
                def two(i, top):
                    j = 2 * i
                    after = score(g, n, j + 1, p0, T, sb)
                    soft(g, n, j, p0, T, sa, top)
                    then = score(g, n, j + 2, p0, T, sa)
                    soft(g, n, j + 1, p0, T, sb, after)
                    return then

                lax.fori_loop(0, (n + 1) // 2, two, score(g, n, 0, p0, T, sa))


def prompt_part(everyone, seg, q0, q1, k, v):
    L = k.shape[0]
    rows, width = q0.shape
    n_resp = everyone.shape[0] * 4
    R = rows // n_resp * 2 * width // HD
    vm = pl.BlockSpec(memory_space=pltpu.VMEM)
    part = jax.ShapeDtypeStruct(q0.shape, BF16)
    stat = jax.ShapeDtypeStruct((rows // UNIT * 8, HD), F32)
    sizes = tuple(L * i // 4 for i in (1, 2, 3, 4))
    return pl.pallas_call(
        functools.partial(prompt_kernel, sizes),
        out_shape=(part, part, stat, stat),
        in_specs=[vm] * 6,
        out_specs=(vm,) * 4,
        scratch_shapes=[
            pltpu.SMEM((G * n_resp,), jnp.int32),
            pltpu.SMEM((G,), jnp.int32),
            pltpu.VMEM((L, R), F32),
            pltpu.VMEM((L, R), F32),
            pltpu.VMEM((HD + ONES, L), BF16),
            pltpu.VMEM((L, 2 * HD), BF16),
            pltpu.SMEM((everyone.shape[0], 1, HD), jnp.int32),
            pltpu.SemaphoreType.DMA,
        ],
        compiler_params=pltpu.CompilerParams(vmem_limit_bytes=20 << 20),
        name="prompt_part",
    )(everyone, seg.reshape(-1, HD), q0, q1, k, v)


def merge(parts):
    top = functools.reduce(jnp.maximum, [st for _, st in parts])
    weights = [jnp.exp2(st - top) for _, st in parts]
    total = functools.reduce(jnp.add, weights)
    scale = 1.0 / total
    turned = [jnp.transpose(w * scale) for w in weights]
    C = UNIT // 2
    lines = []
    for u in range(2):
        line = []
        for h in range(HALF // HD):
            acc = None
            for (o, _), t in zip(parts, turned):
                term = o[u * C : (u + 1) * C, h * HD : (h + 1) * HD].astype(F32) * t[h * C : (h + 1) * C, u : u + 1]
                acc = term if acc is None else acc + term
            line.append(acc)
        lines.append(jnp.concatenate(line, axis=1))
    return jnp.concatenate(lines, axis=0).astype(BF16), top + jnp.log2(total)


class Ring:
    def __init__(self, here, axis, spot, src, in2, in1, out, sems):
        self.here, self.axis, self.spot, self.src, self.in2, self.in1, self.out = here, axis, spot, src, in2, in1, out
        self.send, self.recv = sems
        self.pieces, self.units = in2[0].shape[1], in2[0].shape[2]
        self.started = []

    def copy(self, src, dst, way, kind, p):
        to = self.here.step(self.axis, 1 if way == BACK else -1)
        return [
            remote(a, b, self.send.at[way, kind, p, i], self.recv.at[way, kind, p, i], to)
            for i, (a, b) in enumerate(zip(src, dst))
        ]

    def go(self, copies):
        for c in copies:
            c.start()
            self.started.append(c)

    def line(self, by, group, p):
        return [ref.at[self.here.index(self.axis, by), self.spot(group, p)] for ref in self.src]

    def got(self, way, group, p):
        return [ref.at[way, group * self.pieces + p] for ref in self.in1]

    def begin_far(self, p):
        for way in (BACK, AHEAD):
            self.go(self.copy(self.line(2, way, p), [ref.at[way, p] for ref in self.in2], way, 0, p))

    def begin_near(self, way, p):
        by = 1 if way == BACK else -1
        self.go(self.copy(self.line(by, 1 - way, p), self.got(way, 1 - way, p), way, 1, p))

    def pass_on(self, way, p):
        landed = [ref.at[way, p] for ref in self.in2]
        for c in self.copy(landed, landed, way, 0, p):
            c.wait_recv()
        i, spot = self.here.index(self.axis, 1 if way == BACK else -1), self.spot(way, p)
        for u in range(self.units):
            mine = [ref[i, spot, u] for ref in self.src]
            theirs = [ref[way, p, u] for ref in self.in2]
            for ref, value in zip(self.out, self.join([mine, theirs])):
                ref[way, p, u] = value
        self.go(self.copy([ref.at[way, p] for ref in self.out], self.got(way, way, p), way, 2, p))

    def arrive(self, group, p):
        for way in (BACK, AHEAD):
            refs = self.got(way, group, p)
            for c in self.copy(refs, refs, way, 2 if way == group else 1, p):
                c.wait_recv()

    def total(self, group, p, u, extra=()):
        i, spot = self.here.index(self.axis), self.spot(group, p)
        parts = [[ref[i, spot, u] for ref in self.src]]
        parts += [[ref[way, group * self.pieces + p, u] for ref in self.in1] for way in (BACK, AHEAD)]
        return self.join(parts + list(extra))

    def join(self, parts):
        return merge(parts)

    def finish(self):
        for c in self.started:
            c.wait_send()


class PlainRing(Ring):
    def join(self, parts):
        return [functools.reduce(jnp.add, [p[0].astype(F32) for p in parts]).astype(BF16)]


ROUNDS = (
    ((0, 0), (0, -1), (0, 1), (-1, 0)),
    ((1, 0), (-1, -1), (1, -1), (-1, 1)),
    ((1, 1), (0, 2), (2, 0), (-1, 2)),
    ((1, 2), (2, -1), (2, 1), (2, 2)),
)


def choose(index, values):
    out = jnp.int32(values[0])
    for i in range(1, len(values)):
        out = jnp.where(index == i, values[i], out)
    return out


def project_kernel(
    o0, o1, st0, st1, own_o, own_st, weight, result,
    a_in2, a_in2s, a_in1, a_in1s, a_out, a_outs, a_sum, a_sums,
    b_in2, b_in2s, b_in1, b_in1s, b_out, b_outs,
    att, full0, full1, part, swapped, sums, x_in2, x_in1, x_out, final,
    a_send, a_recv, b_send, b_recv, x_send, x_recv,
    near_send, near_recv, far_send, far_recv, core_send, core_recv, last_send, last_recv, local,
):
    here = Place()
    s, r = here.s, here.r
    x, core = here.at["x"], here.at["core"]
    mate = here.step("core", 1)
    barrier = pltpu.get_barrier_semaphore()
    near = [here.step(axis, by) for axis in ("y", "z", "x") for by in (1, -1)] + [mate]
    for d in near:
        pl.semaphore_signal(barrier, inc=1, device_id=d, device_id_type=MESH)
    targets = []
    for owners in ROUNDS:
        dy, dz = choose(x, [o[0] for o in owners]), choose(x, [o[1] for o in owners])
        targets.append((here.index("y", dy) * SIDE + here.index("z", dz), s // 2))
    spots = {(dy % SIDE) * SIDE + dz % SIDE: j for owners in ROUNDS for j, (dy, dz) in enumerate(owners)}
    sources = []
    for j in range(2):
        sender = 2 * r + j
        dy, dz = (s // SIDE - sender // SIDE + SIDE) % SIDE, (s % SIDE - sender % SIDE + SIDE) % SIDE
        column = choose(dy * SIDE + dz, [spots[i] for i in range(SIDE * SIDE)])
        sources.append([(sender, column * 2 + c) for c in range(2)])
    stays = jnp.logical_and(x == 0, s // 2 == r)
    own_column = s % 2

    def keeps(j, c):
        return jnp.logical_and(stays, jnp.logical_and(own_column == j, core == c))

    for j in range(2):
        for c in range(2):

            @pl.when(jnp.logical_not(keeps(j, c)))
            def _(j=j, c=c):
                pl.semaphore_signal(barrier, inc=1, device_id=sources[j][c], device_id_type=MESH)

    pl.semaphore_wait(barrier, len(near) + len(ROUNDS) - stays.astype(jnp.int32))

    o, st = (o0, o1), (st0, st1)
    one, two = [], []
    order = ((2, 0), (1, -1))
    for X in (0, 1):
        spot = lambda way, p, X=X: here.index(AXES[X][1], order[way][p])
        one.append(
            Ring(
                here, AXES[X][0], spot, (o[X], st[X]), (a_in2.at[X], a_in2s.at[X]), (a_in1.at[X], a_in1s.at[X]),
                (a_out.at[X], a_outs.at[X]), (a_send.at[X], a_recv.at[X]),
            )
        )
        two.append(
            Ring(
                here, AXES[X][1], lambda way, p: way, (a_sum.at[X], a_sums.at[X]), (b_in2.at[X], b_in2s.at[X]),
                (b_in1.at[X], b_in1s.at[X]), (b_out.at[X], b_outs.at[X]), (b_send.at[X], b_recv.at[X]),
            )
        )

    def settle(group, p):
        for X in (0, 1):
            one[X].arrive(group, p)
            d = one[X].spot(group, p)
            for u in range(2):
                value, stat = one[X].total(group, p, u)
                a_sum[X, d, u, 0] = value
                a_sums[X, d, u, 0] = stat

    both = (0, 1)
    for p in range(2):
        for X in both:
            one[X].begin_far(p)
    for p in range(2):
        for X in both:
            for way in (BACK, AHEAD):
                one[X].begin_near(way, p)
        for way in (BACK, AHEAD):
            for X in both:
                one[X].pass_on(way, p)
    settle(BACK, 0)
    for X in both:
        two[X].begin_far(0)
    settle(AHEAD, 0)
    for X in both:
        two[X].begin_near(BACK, 0)
    settle(AHEAD, 1)
    for X in both:
        two[X].begin_near(AHEAD, 0)
    for way in (BACK, AHEAD):
        for X in both:
            two[X].pass_on(way, 0)
    settle(BACK, 1)
    for X in both:
        for way in (BACK, AHEAD):
            two[X].arrive(way, 0)
            value, _ = two[X].total(way, 0, 0, [(own_o[X, way], own_st[X, way])])
            att[X, way * UNIT : (way + 1) * UNIT, :] = value

    full = (full0, full1)
    steps = gather(here, (att.at[0], att.at[1]), full, near_send, near_recv, far_send, far_recv)
    next(steps)
    for X in (0, 1):
        first, second = AXES[X]
        full[X][here.index(second), here.index(first)] = att[X]

    crossing = {}
    rings = [
        PlainRing(
            here, "x", lambda way, p: way, (sums.at[i],), (x_in2.at[i],), (x_in1.at[i],), (x_out.at[i],),
            (x_send.at[i], x_recv.at[i]),
        )
        for i in range(len(ROUNDS))
    ]

    def terms(i):
        for j, (dy, dz) in enumerate(ROUNDS[i]):
            y, z = here.index("y", dy), here.index("z", dz)
            value = jnp.dot(full0[y, z], weight[:HALF, :], preferred_element_type=F32)
            value += jnp.dot(full1[z, y], weight[HALF:, :], preferred_element_type=F32)
            value = value.astype(BF16)
            for c in range(2):
                part[i, c, j] = value[c * UNIT : (c + 1) * UNIT]
        crossing[i] = remote(part.at[i, 1 - core], swapped.at[i], core_send.at[i], core_recv.at[i], mate)
        crossing[i].start()

    def cross(i):
        crossing[i].wait_recv()
        for j in range(SIDE):
            value = (part[i, core, j].astype(F32) + swapped[i, j].astype(F32)).astype(BF16)
            for way in (BACK, AHEAD):
                sums[i, j, way, 0] = value[way * UNIT // 2 : (way + 1) * UNIT // 2]
        rings[i].begin_far(0)
        for way in (BACK, AHEAD):
            rings[i].begin_near(way, 0)

    def pass_on(i):
        for way in (BACK, AHEAD):
            rings[i].pass_on(way, 0)

    columns = pl.ds(pl.multiple_of(own_column * HALF, HALF), HALF)
    half = pl.ds(pl.multiple_of(core * UNIT, UNIT), UNIT)

    def deliver(i):
        for way in (BACK, AHEAD):
            rings[i].arrive(way, 0)
            final[i, way * UNIT // 2 : (way + 1) * UNIT // 2] = rings[i].total(way, 0, 0)[0]
        copy = remote(
            final.at[i], result.at[half, columns], last_send.at[i], last_recv.at[own_column, core], targets[i]
        )
        if i == 0:
            pl.when(jnp.logical_not(stays))(copy.start)

            @pl.when(stays)
            def _():
                pltpu.make_async_copy(final.at[i], result.at[half, columns], local).start()
        else:
            copy.start()

    plan = {
        "far0": (terms, 0), "far1": (cross, 0), "far2": (terms, 1, pass_on, 0), "far3": (cross, 1, deliver, 0),
        "past1": (terms, 2, pass_on, 1), "past2": (cross, 2, deliver, 1),
        "past3": (terms, 3, pass_on, 2, cross, 3, deliver, 2),
    }
    for stage in steps:
        todo = plan.get(stage, ())
        for k in range(0, len(todo), 2):
            todo[k](todo[k + 1])
    pass_on(3)
    deliver(3)

    for ring in one + two + rings:
        ring.finish()
    for i in range(len(ROUNDS)):
        crossing[i].wait_send()
        copy = remote(
            final.at[i], result.at[half, columns], last_send.at[i], last_recv.at[own_column, core], targets[i]
        )
        if i == 0:
            pl.when(jnp.logical_not(stays))(copy.wait_send)

            @pl.when(stays)
            def _():
                pltpu.make_async_copy(final.at[i], result.at[half, columns], local).wait()
        else:
            copy.wait_send()
    for j in range(2):
        for c in range(2):
            dst = result.at[c * UNIT : (c + 1) * UNIT, j * HALF : (j + 1) * HALF]
            copy = remote(dst, dst, last_send.at[0], last_recv.at[j, c], mate)
            pl.when(jnp.logical_not(keeps(j, c)))(copy.wait_recv)


def project(o0, o1, st0, st1, own_o, own_st, weight):
    vm = pl.BlockSpec(memory_space=pltpu.VMEM)
    dma = pltpu.SemaphoreType.DMA
    block, stat = (UNIT, HALF), (8, HD)
    rows = 2 * UNIT
    rounds = len(ROUNDS)
    o0, o1 = (a.reshape(SIDE, SIDE, 2, *block) for a in (o0, o1))
    st0, st1 = (a.reshape(SIDE, SIDE, 2, *stat) for a in (st0, st1))
    pair = lambda *lead: [pltpu.VMEM(lead + block, BF16), pltpu.VMEM(lead + stat, F32)]
    strip = (UNIT // 2, HALF)
    return pl.pallas_call(
        project_kernel,
        out_shape=jax.ShapeDtypeStruct((rows, 2 * HALF), BF16),
        in_specs=[vm] * 7,
        out_specs=vm,
        scratch_shapes=[
            *pair(2, 2, 2, 2), *pair(2, 2, 4, 2), *pair(2, 2, 2, 2), *pair(2, SIDE, 2, 1),
            *pair(2, 2, 1, 1), *pair(2, 2, 2, 1), *pair(2, 2, 1, 1),
            pltpu.VMEM((2, rows, HALF), BF16),
            pltpu.VMEM((SIDE, SIDE, rows, HALF), BF16),
            pltpu.VMEM((SIDE, SIDE, rows, HALF), BF16),
            pltpu.VMEM((rounds, 2, SIDE) + block, BF16),
            pltpu.VMEM((rounds, SIDE) + block, BF16),
            pltpu.VMEM((rounds, SIDE, 2, 1) + strip, BF16),
            pltpu.VMEM((rounds, 2, 1, 1) + strip, BF16),
            pltpu.VMEM((rounds, 2, 2, 1) + strip, BF16),
            pltpu.VMEM((rounds, 2, 1, 1) + strip, BF16),
            pltpu.VMEM((rounds,) + block, BF16),
            dma((2, 2, 3, 2, 2)), dma((2, 2, 3, 2, 2)), dma((2, 2, 3, 1, 2)), dma((2, 2, 3, 1, 2)),
            dma((rounds, 2, 3, 1, 1)), dma((rounds, 2, 3, 1, 1)),
            dma((2, 2, 2)), dma((2, 2, 2)), dma((2, 2, 8)), dma((2, 2, 8)),
            dma((rounds,)), dma((rounds,)), dma((rounds,)), dma((2, 2)), dma,
        ],
        compiler_params=pltpu.CompilerParams(collective_id=2, has_side_effects=True, vmem_limit_bytes=34 << 20),
        name="merge_and_project",
    )(o0, o1, st0, st1, own_o, own_st, weight)


def per_device(
    queries, prompt_keys, prompt_values, prompt_segment, own_keys, own_values, resp_lengths, resp_groups, out_weight
):
    n, C, width = queries.shape
    q = queries.reshape(n * C, width)
    full0, full1, everyone, own_o, own_st = spread(resp_lengths, resp_groups, q, own_keys, own_values)
    flat = lambda a: a.reshape(-1, HALF)
    parts = prompt_part(everyone, prompt_segment, flat(full0), flat(full1), prompt_keys, prompt_values)
    return project(*parts, own_o, own_st, out_weight).reshape(n, C, width)


def solution(mesh):
    in_specs = (
        P("seq", None, "resp"),
        P("seq", "resp"),
        P("seq", "resp"),
        P("seq"),
        P("seq", None, "resp"),
        P("seq", None, "resp"),
        P("seq"),
        P("seq"),
        P("resp", "seq"),
    )
    return jax.shard_map(
        per_device, mesh=mesh, in_specs=in_specs, out_specs=P("seq", None, "resp"), check_vma=False
    )
```

```python
import functools
import math

import jax
import jax.numpy as jnp
from jax import lax
from jax.experimental import pallas as pl
from jax.experimental.pallas import tpu as pltpu
from jax.sharding import PartitionSpec as P

HD = 128
G = 4
SIDE = 4
NEG = -1e30
C2 = math.log2(math.e) / math.sqrt(HD)
ONES = 16
HALF = 512
UNIT = 64
MESH = pl.DeviceIdType.MESH
BF16 = jnp.bfloat16
F32 = jnp.float32


class Place:
    def __init__(self):
        s, r = lax.axis_index("seq"), lax.axis_index("resp")
        self.s, self.r = s, r
        self.at = {"y": s // SIDE, "z": s % SIDE, "x": r // 2, "core": r % 2}

    def step(self, axis, by):
        c = dict(self.at)
        c[axis] = (c[axis] + by + SIDE) % SIDE if axis != "core" else 1 - c[axis]
        return (c["y"] * SIDE + c["z"], c["x"] * 2 + c["core"])

    def index(self, axis, by=0):
        return (self.at[axis] + by + SIDE) % SIDE


AXES = (("z", "y"), ("y", "z"))
BACK, AHEAD = 0, 1


def remote(src, dst, send, recv, to):
    return pltpu.make_async_remote_copy(
        src_ref=src, dst_ref=dst, send_sem=send, recv_sem=recv, device_id=to, device_id_type=MESH
    )


def gather(here, mine, full, near_send, near_recv, far_send, far_recv):
    started = []
    orders = (0, -1, 1, 2)

    def go(copy):
        copy.start()
        started.append(copy)

    def near(X, src, dst, way, kind):
        to = here.step(AXES[X][0], 1 if way == BACK else -1)
        return remote(src, dst, near_send.at[X, way, kind], near_recv.at[X, way, kind], to)

    def far(X, src, dst, way, kind):
        to = here.step(AXES[X][1], 1 if way == BACK else -1)
        return remote(src, dst, far_send.at[X, way, kind], far_recv.at[X, way, kind], to)

    def slot(X, by2, by1):
        first, second = AXES[X]
        return full[X].at[here.index(second, by2), here.index(first, by1)]

    def along(X, k):
        ref = mine[X] if k == 0 else slot(X, 0, orders[k])
        for way in (BACK, AHEAD):
            go(far(X, ref, slot(X, 0, orders[k]), way, k))

    def landed(k):
        for X in (0, 1):
            for way in (BACK, AHEAD):
                ref = slot(X, -1 if way == BACK else 1, orders[k])
                far(X, ref, ref, way, k).wait_recv()
                if way == (BACK if k < 2 else AHEAD):
                    go(far(X, ref, ref, way, 4 + k))

    top, low = pl.ds(0, UNIT), pl.ds(UNIT, UNIT)
    for X in (0, 1):
        for way in (BACK, AHEAD):
            go(near(X, mine[X], slot(X, 0, 0), way, 0))
    for X in (0, 1):
        along(X, 0)
    yield "sent"
    for way, by, part in ((BACK, -1, top), (AHEAD, 1, low)):
        for X in (0, 1):
            ref = slot(X, 0, by)
            near(X, ref, ref, way, 0).wait_recv()
            go(near(X, ref.at[part], ref.at[part], way, 1))
            along(X, 1 if way == BACK else 2)
    yield "near"
    landed(0)
    yield "far0"
    for X in (0, 1):
        ref = slot(X, 0, 2)
        near(X, ref.at[top], ref.at[top], BACK, 1).wait_recv()
        near(X, ref.at[low], ref.at[low], AHEAD, 1).wait_recv()
        along(X, 3)
    yield "line"
    for k in (1, 2, 3):
        landed(k)
        yield "far" + str(k)
    for k in (0, 1, 2, 3):
        for X in (0, 1):
            ref = slot(X, 2, orders[k])
            far(X, ref, ref, BACK if k < 2 else AHEAD, 4 + k).wait_recv()
        yield "past" + str(k)
    for copy in started:
        copy.wait_send()


def greet(devices, count):
    barrier = pltpu.get_barrier_semaphore()
    for d in devices:
        pl.semaphore_signal(barrier, inc=1, device_id=d, device_id_type=MESH)
    pl.semaphore_wait(barrier, count)


def heads_first(ref, base, rows, heads):
    return jnp.concatenate([ref[pl.ds(base, rows), h * HD : (h + 1) * HD] for h in range(heads)], axis=0)


def transpose_values(v):
    return jnp.transpose(v.astype(F32)).astype(BF16)


def spread_kernel(
    lengths, groups, q, keys, values,
    full0, full1, everyone, own_o, own_st,
    qbuf, kbuf, vbuf, lens, marks, scores, vt, tile,
    near_send, near_recv, far_send, far_recv, group_send, group_recv, load,
):
    here = Place()
    s, r = here.s, here.r
    n, hist, _ = keys.shape
    C = q.shape[0] // n
    H = q.shape[1] // HD
    rows = C * H
    seqs = SIDE * SIDE
    loads = [
        pltpu.make_async_copy(src, dst, load.at[i])
        for i, (src, dst) in enumerate(((groups, marks), (lengths, lens), (q, qbuf), (keys, kbuf), (values, vbuf)))
    ]
    for copy in loads:
        copy.start()
    others = [((s + d) % seqs, r) for d in range(1, seqs)]
    greet(others, seqs - 1)
    mine = [q.at[:, X * HALF : (X + 1) * HALF] for X in (0, 1)]
    full = (full0, full1)
    steps = gather(here, mine, full, near_send, near_recv, far_send, far_recv)
    next(steps)
    loads[0].wait()
    lane = lax.broadcasted_iota(jnp.int32, tile.shape, 1)
    mark = jnp.zeros(tile.shape, jnp.int32)
    for i in range(n):
        mark = jnp.where(lane == i, marks[i], mark)
    tile[...] = mark
    told = []
    for d, to in enumerate(others):
        copy = remote(tile, everyone.at[s], group_send.at[d], group_recv.at[d], to)
        copy.start()
        told.append(copy)
    for copy in loads[1:]:
        copy.wait()
    for X in (0, 1):
        first, second = AXES[X]
        full[X][here.index(second), here.index(first)] = qbuf[:, X * HALF : (X + 1) * HALF]
    everyone[s] = mark
    own_st[...] = jnp.full(own_st.shape, NEG, F32)
    vt[HD:, :] = jnp.ones((ONES, hist), BF16)

    def own(u, _):
        base = pl.multiple_of(u * C, C)
        qa = heads_first(qbuf, base, C, H)
        sc = lax.dot_general(kbuf[u], qa, (((1,), (1,)), ((), ())), preferred_element_type=F32)
        pos = lax.broadcasted_iota(jnp.int32, (hist, rows), 0)
        upto = lens[u] + lax.broadcasted_iota(jnp.int32, (1, rows), 1) % C
        sc = jnp.where(pos <= upto, sc, NEG)
        scores[...] = sc
        for j in range(0, hist, HD):
            vt[:HD, j : j + HD] = transpose_values(vbuf[u, j : j + HD, :])
        shift = jnp.max(sc, axis=0, keepdims=True) * C2
        p = jnp.exp2(scores[...] * C2 - shift).astype(BF16)
        out = jnp.dot(vt[...], p, preferred_element_type=F32)
        total = out[HD : HD + 1, :]
        lse = shift + jnp.log2(total)
        out = out[:HD, :] * (1.0 / total)
        for X in (0, 1):
            own_st[X, u // 2, pl.ds(u % 2, 1), :] = lse[:, X * HD : (X + 1) * HD]
            t = jnp.transpose(out[:, X * HD : (X + 1) * HD])
            for w in range(HD // C):
                own_o[X, u // 2, pl.ds(pl.multiple_of(u % 2 * C, C), C), w * HD : (w + 1) * HD] = t[w * C : (w + 1) * C, :]
        return 0

    lax.fori_loop(0, n // 2, own, 0)
    for stage in steps:
        if stage == "far0":
            lax.fori_loop(n // 2, n, own, 0)
    for d, copy in enumerate(told):
        copy.wait_send()
        src = everyone.at[(s + seqs - 1 - d) % seqs]
        remote(src, src, group_send.at[d], group_recv.at[d], others[d]).wait_recv()


def spread(lengths, groups, q, keys, values):
    n, hist, _ = keys.shape
    C = q.shape[0] // n
    rows = C * q.shape[1] // HD
    vm, hbm = (pl.BlockSpec(memory_space=m) for m in (pltpu.VMEM, pltpu.HBM))
    dma = pltpu.SemaphoreType.DMA
    full = jax.ShapeDtypeStruct((SIDE, SIDE, n * C, HALF), BF16)
    return pl.pallas_call(
        spread_kernel,
        out_shape=(
            full,
            full,
            jax.ShapeDtypeStruct((SIDE * SIDE, 8, HD), jnp.int32),
            jax.ShapeDtypeStruct((2, 2, UNIT, HALF), F32),
            jax.ShapeDtypeStruct((2, 2, 8, HD), F32),
        ),
        in_specs=[hbm] * 5,
        out_specs=(vm,) * 5,
        scratch_shapes=[
            pltpu.VMEM(q.shape, BF16),
            pltpu.VMEM(keys.shape, BF16),
            pltpu.VMEM(keys.shape, BF16),
            pltpu.SMEM((n,), jnp.int32),
            pltpu.SMEM((n,), jnp.int32),
            pltpu.VMEM((hist, rows), F32),
            pltpu.VMEM((HD + ONES, hist), BF16),
            pltpu.VMEM((8, HD), jnp.int32),
            dma((2, 2, 2)), dma((2, 2, 2)), dma((2, 2, 8)), dma((2, 2, 8)),
            dma((SIDE * SIDE - 1,)), dma((SIDE * SIDE - 1,)), dma((5,)),
        ],
        compiler_params=pltpu.CompilerParams(collective_id=1, has_side_effects=True, vmem_limit_bytes=24 << 20),
        name="spread_queries",
    )(*(pltpu.with_memory_space_constraint(a, pltpu.HBM) for a in (lengths, groups, q, keys, values)))


def prompt_kernel(sizes, everyone, seg, q0, q1, k, v, o0, o1, st0, st1, lists, count, sa, sb, vt, ka, groups, load):
    fetch = pltpu.make_async_copy(everyone.at[:, 0:1], groups, load)
    fetch.start()
    n_resp = everyone.shape[0] * 4
    C = q0.shape[0] // n_resp
    H = 2 * HALF // HD
    L = k.shape[0]
    rows = C * H
    per = 4
    for ref in (st0, st1):
        ref[...] = jnp.full(ref.shape, NEG, F32)
    for ref in (o0, o1):
        ref[...] = jnp.zeros(ref.shape, BF16)
    for j in range(0, L, HD):
        vt[:HD, j : j + HD] = transpose_values(v[j : j + HD, :])
    vt[HD:, :] = jnp.ones((ONES, L), BF16)
    sg = seg[...]
    cut = [jnp.int32(0)] + [jnp.sum((sg < g).astype(jnp.int32)) for g in range(1, G)] + [jnp.int32(L)]
    lane = lax.broadcasted_iota(jnp.int32, (1, HD), 1)
    low, high = jnp.zeros((1, HD), jnp.int32), jnp.full((1, HD), L, jnp.int32)
    for g in range(G):
        low = jnp.where(lane == g, cut[g], low)
        high = jnp.where(lane == g, cut[g + 1], high)
        count[g] = 0
    ka[:, :HD] = k[...]
    pos = lax.broadcasted_iota(jnp.int32, (L, HD), 0)
    ka[:, HD:] = jnp.where(jnp.logical_and(pos >= low, pos < high), 0.0, NEG).astype(BF16)

    def scan(r, _):
        g = groups[r // per, 0, r % per]
        c = count[g]
        lists[g * n_resp + c] = r
        count[g] = c + 1
        return 0

    fetch.wait()
    lax.fori_loop(0, n_resp, scan, 0)

    def spots(r):
        s, u = r // per, r % per
        turned = (s % SIDE) * SIDE + s // SIDE
        return s, turned, u

    def score(g, n, i, p0, T, dst):
        s, turned, u = spots(lists[g * n_resp + jnp.minimum(i, n - 1)])
        base0 = pl.multiple_of((s * per + u) * C, C)
        base1 = pl.multiple_of((turned * per + u) * C, C)
        mine = jnp.concatenate([heads_first(q0, base0, C, H // 2), heads_first(q1, base1, C, H // 2)], axis=0)
        flag = (lax.broadcasted_iota(jnp.int32, (rows, HD), 1) == g).astype(F32).astype(BF16)
        qa = jnp.concatenate([mine, flag], axis=1)
        sc = lax.dot_general(ka[pl.ds(p0, T), :], qa, (((1,), (1,)), ((), ())), preferred_element_type=F32)
        dst[:T, :] = sc
        return jnp.max(sc, axis=0, keepdims=True)

    def soft(g, n, i, p0, T, src, top):
        s, turned, u = spots(lists[g * n_resp + jnp.minimum(i, n - 1)])
        shift = top * C2
        p = jnp.exp2(src[:T, :] * C2 - shift).astype(BF16)
        out = jnp.dot(vt[:, pl.ds(p0, T)], p, preferred_element_type=F32)
        total = out[HD : HD + 1, :]
        lse = shift + jnp.log2(total)
        out = out[:HD, :] * (1.0 / total)
        for X, o, st, place in ((0, o0, st0, turned), (1, o1, st1, s)):
            st[pl.ds((place * 2 + u // 2) * 8 + u % 2, 1), :] = lse[:, X * HD : (X + 1) * HD]
            base = pl.multiple_of((place * per + u) * C, C)
            t = jnp.transpose(out[:, X * HD : (X + 1) * HD]).astype(BF16)
            for w in range(HD // C):
                o[pl.ds(base, C), w * HD : (w + 1) * HD] = t[w * C : (w + 1) * C, :]

    for g in range(G):
        lo, hi, n = cut[g], cut[g + 1], count[g]
        start = lo // HD * HD
        for T, less in zip(sizes, (0,) + sizes[:-1]):
            p0 = pl.multiple_of(jnp.minimum(start, L - T), HD)
            fits = hi - p0 <= T
            if less:
                fits = jnp.logical_and(fits, hi - jnp.minimum(start, L - less) > less)

            @pl.when(jnp.logical_and(jnp.logical_and(hi > lo, n > 0), fits))
            def _(T=T, p0=p0, n=n, g=g):
                def two(i, top):
                    j = 2 * i
                    after = score(g, n, j + 1, p0, T, sb)
                    soft(g, n, j, p0, T, sa, top)
                    then = score(g, n, j + 2, p0, T, sa)
                    soft(g, n, j + 1, p0, T, sb, after)
                    return then

                lax.fori_loop(0, (n + 1) // 2, two, score(g, n, 0, p0, T, sa))


def prompt_part(everyone, seg, q0, q1, k, v):
    L = k.shape[0]
    rows, width = q0.shape
    n_resp = everyone.shape[0] * 4
    R = rows // n_resp * 2 * width // HD
    vm = pl.BlockSpec(memory_space=pltpu.VMEM)
    part = jax.ShapeDtypeStruct(q0.shape, BF16)
    stat = jax.ShapeDtypeStruct((rows // UNIT * 8, HD), F32)
    sizes = tuple(L * i // 4 for i in (1, 2, 3, 4))
    return pl.pallas_call(
        functools.partial(prompt_kernel, sizes),
        out_shape=(part, part, stat, stat),
        in_specs=[vm] * 6,
        out_specs=(vm,) * 4,
        scratch_shapes=[
            pltpu.SMEM((G * n_resp,), jnp.int32),
            pltpu.SMEM((G,), jnp.int32),
            pltpu.VMEM((L, R), F32),
            pltpu.VMEM((L, R), F32),
            pltpu.VMEM((HD + ONES, L), BF16),
            pltpu.VMEM((L, 2 * HD), BF16),
            pltpu.SMEM((everyone.shape[0], 1, HD), jnp.int32),
            pltpu.SemaphoreType.DMA,
        ],
        compiler_params=pltpu.CompilerParams(vmem_limit_bytes=20 << 20),
        name="prompt_part",
    )(everyone, seg.reshape(-1, HD), q0, q1, k, v)


def merge(parts):
    top = functools.reduce(jnp.maximum, [st for _, st in parts])
    weights = [jnp.exp2(st - top) for _, st in parts]
    total = functools.reduce(jnp.add, weights)
    scale = 1.0 / total
    turned = [jnp.transpose(w * scale) for w in weights]
    C = UNIT // 2
    lines = []
    for u in range(2):
        line = []
        for h in range(HALF // HD):
            acc = None
            for (o, _), t in zip(parts, turned):
                term = o[u * C : (u + 1) * C, h * HD : (h + 1) * HD].astype(F32) * t[h * C : (h + 1) * C, u : u + 1]
                acc = term if acc is None else acc + term
            line.append(acc)
        lines.append(jnp.concatenate(line, axis=1))
    return jnp.concatenate(lines, axis=0).astype(BF16), top + jnp.log2(total)


class Ring:
    def __init__(self, here, axis, spot, src, in2, in1, out, sems):
        self.here, self.axis, self.spot, self.src, self.in2, self.in1, self.out = here, axis, spot, src, in2, in1, out
        self.send, self.recv = sems
        self.pieces, self.units = in2[0].shape[1], in2[0].shape[2]
        self.started = []

    def copy(self, src, dst, way, kind, p):
        to = self.here.step(self.axis, 1 if way == BACK else -1)
        return [
            remote(a, b, self.send.at[way, kind, p, i], self.recv.at[way, kind, p, i], to)
            for i, (a, b) in enumerate(zip(src, dst))
        ]

    def go(self, copies):
        for c in copies:
            c.start()
            self.started.append(c)

    def line(self, by, group, p):
        return [ref.at[self.here.index(self.axis, by), self.spot(group, p)] for ref in self.src]

    def got(self, way, group, p):
        return [ref.at[way, group * self.pieces + p] for ref in self.in1]

    def begin_far(self, p):
        for way in (BACK, AHEAD):
            self.go(self.copy(self.line(2, way, p), [ref.at[way, p] for ref in self.in2], way, 0, p))

    def begin_near(self, way, p):
        by = 1 if way == BACK else -1
        self.go(self.copy(self.line(by, 1 - way, p), self.got(way, 1 - way, p), way, 1, p))

    def pass_on(self, way, p):
        landed = [ref.at[way, p] for ref in self.in2]
        for c in self.copy(landed, landed, way, 0, p):
            c.wait_recv()
        i, spot = self.here.index(self.axis, 1 if way == BACK else -1), self.spot(way, p)
        for u in range(self.units):
            mine = [ref[i, spot, u] for ref in self.src]
            theirs = [ref[way, p, u] for ref in self.in2]
            for ref, value in zip(self.out, merge([mine, theirs])):
                ref[way, p, u] = value
        self.go(self.copy([ref.at[way, p] for ref in self.out], self.got(way, way, p), way, 2, p))

    def arrive(self, group, p):
        for way in (BACK, AHEAD):
            refs = self.got(way, group, p)
            for c in self.copy(refs, refs, way, 2 if way == group else 1, p):
                c.wait_recv()

    def total(self, group, p, u, extra=()):
        i, spot = self.here.index(self.axis), self.spot(group, p)
        parts = [[ref[i, spot, u] for ref in self.src]]
        parts += [[ref[way, group * self.pieces + p, u] for ref in self.in1] for way in (BACK, AHEAD)]
        return merge(parts + list(extra))

    def finish(self):
        for c in self.started:
            c.wait_send()


ROUNDS = (
    ((0, 0), (0, -1), (0, 1), (-1, 0)),
    ((1, 0), (-1, -1), (1, -1), (-1, 1)),
    ((1, 1), (0, 2), (2, 0), (-1, 2)),
    ((1, 2), (2, -1), (2, 1), (2, 2)),
)


def choose(index, values):
    out = jnp.int32(values[0])
    for i in range(1, len(values)):
        out = jnp.where(index == i, values[i], out)
    return out


def project_kernel(
    o0, o1, st0, st1, own_o, own_st, weight, result,
    a_in2, a_in2s, a_in1, a_in1s, a_out, a_outs, a_sum, a_sums,
    b_in2, b_in2s, b_in1, b_in1s, b_out, b_outs,
    att, full0, full1, part, swapped, sums, x_in, final, moved,
    a_send, a_recv, b_send, b_recv, x_send, x_recv,
    near_send, near_recv, far_send, far_recv, core_send, core_recv, move_send, move_recv, last_send, last_recv, local,
):
    here = Place()
    s, r = here.s, here.r
    x, core = here.at["x"], here.at["core"]
    mate = here.step("core", 1)
    steps_to = [[choose(x, [o[k] for o in owners]) for k in (0, 1)] for owners in ROUNDS]

    def beside(i, sign):
        dy, dz = steps_to[i]
        return here.index("y", sign * dy), here.index("z", sign * dz)

    still = x == 0

    def moves(i, act):
        if i == 0:
            pl.when(jnp.logical_not(still))(act)
        else:
            act()

    row = [(s, (r + d) % (2 * SIDE)) for d in range(1, 2 * SIDE)]
    barrier = pltpu.get_barrier_semaphore()
    for d in [here.step(axis, by) for axis in ("y", "z") for by in (1, -1)] + row:
        pl.semaphore_signal(barrier, inc=1, device_id=d, device_id_type=MESH)
    for i in range(len(ROUNDS)):
        y, z = beside(i, -1)
        moves(i, lambda: pl.semaphore_signal(barrier, inc=1, device_id=(y * SIDE + z, r), device_id_type=MESH))
    pl.semaphore_wait(barrier, 4 + len(row) + len(ROUNDS) - still.astype(jnp.int32))

    o, st = (o0, o1), (st0, st1)
    one, two = [], []
    order = ((2, 0), (1, -1))
    for X in (0, 1):
        spot = lambda way, p, X=X: here.index(AXES[X][1], order[way][p])
        one.append(
            Ring(
                here, AXES[X][0], spot, (o[X], st[X]), (a_in2.at[X], a_in2s.at[X]), (a_in1.at[X], a_in1s.at[X]),
                (a_out.at[X], a_outs.at[X]), (a_send.at[X], a_recv.at[X]),
            )
        )
        two.append(
            Ring(
                here, AXES[X][1], lambda way, p: way, (a_sum.at[X], a_sums.at[X]), (b_in2.at[X], b_in2s.at[X]),
                (b_in1.at[X], b_in1s.at[X]), (b_out.at[X], b_outs.at[X]), (b_send.at[X], b_recv.at[X]),
            )
        )

    def settle(group, p):
        for X in (0, 1):
            one[X].arrive(group, p)
            d = one[X].spot(group, p)
            for u in range(2):
                value, stat = one[X].total(group, p, u)
                a_sum[X, d, u, 0] = value
                a_sums[X, d, u, 0] = stat

    both = (0, 1)
    for p in range(2):
        for X in both:
            one[X].begin_far(p)
    for p in range(2):
        for X in both:
            for way in (BACK, AHEAD):
                one[X].begin_near(way, p)
        for way in (BACK, AHEAD):
            for X in both:
                one[X].pass_on(way, p)
    settle(BACK, 0)
    for X in both:
        two[X].begin_far(0)
    settle(AHEAD, 0)
    for X in both:
        two[X].begin_near(BACK, 0)
    settle(AHEAD, 1)
    for X in both:
        two[X].begin_near(AHEAD, 0)
    for way in (BACK, AHEAD):
        for X in both:
            two[X].pass_on(way, 0)
    settle(BACK, 1)
    for X in both:
        for way in (BACK, AHEAD):
            two[X].arrive(way, 0)
            value, _ = two[X].total(way, 0, 0, [(own_o[X, way], own_st[X, way])])
            att[X, way * UNIT : (way + 1) * UNIT, :] = value

    full = (full0, full1)
    steps = gather(here, (att.at[0], att.at[1]), full, near_send, near_recv, far_send, far_recv)
    next(steps)
    for X in (0, 1):
        first, second = AXES[X]
        full[X][here.index(second), here.index(first)] = att[X]

    crossing = {}

    def terms(i):
        for j, (dy, dz) in enumerate(ROUNDS[i]):
            y, z = here.index("y", dy), here.index("z", dz)
            value = jnp.dot(full0[y, z], weight[:HALF, :], preferred_element_type=F32)
            value += jnp.dot(full1[z, y], weight[HALF:, :], preferred_element_type=F32)
            value = value.astype(BF16)
            for c in range(2):
                part[i, c, j] = value[c * UNIT : (c + 1) * UNIT]
        crossing[i] = remote(part.at[i, 1 - core], swapped.at[i], core_send.at[i], core_recv.at[i], mate)
        crossing[i].start()

    def shift(i, d):
        j = here.index("x", d)
        return remote(sums.at[i, j], x_in.at[i, d - 1], x_send.at[i, d - 1], x_recv.at[i, d - 1], here.step("x", d))

    def cross(i):
        crossing[i].wait_recv()
        for d in (2, 1, 3, 0):
            j = here.index("x", d)
            sums[i, j] = (part[i, core, j].astype(F32) + swapped[i, j].astype(F32)).astype(BF16)
            if d:
                shift(i, d).start()

    def move(i):
        y, z = beside(i, 1)
        return remote(final.at[i], moved.at[i], move_send.at[i], move_recv.at[i], (y * SIDE + z, r))

    def deliver(i):
        for d in (1, 2, 3):
            shift(i, d).wait_recv()
        value = sums[i, x].astype(F32)
        for d in (1, 2, 3):
            value += x_in[i, d - 1].astype(F32)
        value = value.astype(BF16)
        final[i] = value
        moves(i, lambda: move(i).start())
        if i == 0:

            @pl.when(still)
            def _():
                moved[i] = value

    def last(i):
        y, z = beside(i, -1)
        owner = y * 2 + z // 2
        dst = result.at[
            pl.ds(pl.multiple_of(core * UNIT, UNIT), UNIT), pl.ds(pl.multiple_of(z % 2 * HALF, HALF), HALF)
        ]
        away = remote(moved.at[i], dst, last_send.at[i], last_recv.at[z % 2, core], (s, owner))
        return away, pltpu.make_async_copy(moved.at[i], dst, local.at[i]), owner == r

    def forward(i):
        moves(i, lambda: move(i).wait_recv())
        away, home, stays = last(i)
        pl.when(jnp.logical_not(stays))(away.start)
        pl.when(stays)(home.start)

    plan = {
        "far0": (terms, 0), "far1": (cross, 0), "far2": (terms, 1, deliver, 0), "far3": (cross, 1, forward, 0),
        "past1": (terms, 2, deliver, 1), "past2": (cross, 2, forward, 1),
        "past3": (terms, 3, deliver, 2, cross, 3, forward, 2),
    }
    for stage in steps:
        todo = plan.get(stage, ())
        for k in range(0, len(todo), 2):
            todo[k](todo[k + 1])
    deliver(3)
    forward(3)

    for ring in one + two:
        ring.finish()
    for i in range(len(ROUNDS)):
        crossing[i].wait_send()
        for d in (1, 2, 3):
            shift(i, d).wait_send()
        moves(i, lambda: move(i).wait_send())
        away, home, stays = last(i)
        pl.when(jnp.logical_not(stays))(away.wait_send)
        pl.when(stays)(home.wait)
    spots = {(dy % SIDE) * SIDE + dz % SIDE: j for owners in ROUNDS for j, (dy, dz) in enumerate(owners)}
    for j in range(2):
        sender = 2 * r + j
        dy, dz = here.index("y", -(sender // SIDE)), here.index("z", -(sender % SIDE))
        column = choose(dy * SIDE + dz, [spots[i] for i in range(SIDE * SIDE)])
        for c in range(2):
            dst = result.at[c * UNIT : (c + 1) * UNIT, j * HALF : (j + 1) * HALF]
            copy = remote(dst, dst, last_send.at[0], last_recv.at[j, c], mate)
            pl.when(jnp.logical_not(jnp.logical_and(column == x, core == c)))(copy.wait_recv)


def project(o0, o1, st0, st1, own_o, own_st, weight):
    vm = pl.BlockSpec(memory_space=pltpu.VMEM)
    dma = pltpu.SemaphoreType.DMA
    block, stat = (UNIT, HALF), (8, HD)
    rows = 2 * UNIT
    rounds = len(ROUNDS)
    o0, o1 = (a.reshape(SIDE, SIDE, 2, *block) for a in (o0, o1))
    st0, st1 = (a.reshape(SIDE, SIDE, 2, *stat) for a in (st0, st1))
    pair = lambda *lead: [pltpu.VMEM(lead + block, BF16), pltpu.VMEM(lead + stat, F32)]
    return pl.pallas_call(
        project_kernel,
        out_shape=jax.ShapeDtypeStruct((rows, 2 * HALF), BF16),
        in_specs=[vm] * 7,
        out_specs=vm,
        scratch_shapes=[
            *pair(2, 2, 2, 2), *pair(2, 2, 4, 2), *pair(2, 2, 2, 2), *pair(2, SIDE, 2, 1),
            *pair(2, 2, 1, 1), *pair(2, 2, 2, 1), *pair(2, 2, 1, 1),
            pltpu.VMEM((2, rows, HALF), BF16),
            pltpu.VMEM((SIDE, SIDE, rows, HALF), BF16),
            pltpu.VMEM((SIDE, SIDE, rows, HALF), BF16),
            pltpu.VMEM((rounds, 2, SIDE) + block, BF16),
            pltpu.VMEM((rounds, SIDE) + block, BF16),
            pltpu.VMEM((rounds, SIDE) + block, BF16),
            pltpu.VMEM((rounds, SIDE - 1) + block, BF16),
            pltpu.VMEM((rounds,) + block, BF16),
            pltpu.VMEM((rounds,) + block, BF16),
            dma((2, 2, 3, 2, 2)), dma((2, 2, 3, 2, 2)), dma((2, 2, 3, 1, 2)), dma((2, 2, 3, 1, 2)),
            dma((rounds, SIDE - 1)), dma((rounds, SIDE - 1)),
            dma((2, 2, 2)), dma((2, 2, 2)), dma((2, 2, 8)), dma((2, 2, 8)),
            dma((rounds,)), dma((rounds,)), dma((rounds,)), dma((rounds,)), dma((rounds,)), dma((2, 2)), dma((rounds,)),
        ],
        compiler_params=pltpu.CompilerParams(collective_id=2, has_side_effects=True, vmem_limit_bytes=34 << 20),
        name="merge_and_project",
    )(o0, o1, st0, st1, own_o, own_st, weight)


def per_device(
    queries, prompt_keys, prompt_values, prompt_segment, own_keys, own_values, resp_lengths, resp_groups, out_weight
):
    n, C, width = queries.shape
    q = queries.reshape(n * C, width)
    full0, full1, everyone, own_o, own_st = spread(resp_lengths, resp_groups, q, own_keys, own_values)
    flat = lambda a: a.reshape(-1, HALF)
    parts = prompt_part(everyone, prompt_segment, flat(full0), flat(full1), prompt_keys, prompt_values)
    return project(*parts, own_o, own_st, out_weight).reshape(n, C, width)


def solution(mesh):
    in_specs = (
        P("seq", None, "resp"),
        P("seq", "resp"),
        P("seq", "resp"),
        P("seq"),
        P("seq", None, "resp"),
        P("seq", None, "resp"),
        P("seq"),
        P("seq"),
        P("resp", "seq"),
    )
    return jax.shard_map(
        per_device, mesh=mesh, in_specs=in_specs, out_specs=P("seq", None, "resp"), check_vma=False
    )
```

```python
import functools
import math

import jax
import jax.numpy as jnp
from jax import lax
from jax.experimental import pallas as pl
from jax.experimental.pallas import tpu as pltpu
from jax.sharding import PartitionSpec as P

HD = 128
G = 4
SIDE = 4
NEG = -1e30
C2 = math.log2(math.e) / math.sqrt(HD)
ONES = 16
HALF = 512
UNIT = 64
MESH = pl.DeviceIdType.MESH
BF16 = jnp.bfloat16
F32 = jnp.float32


class Place:
    def __init__(self):
        s, r = lax.axis_index("seq"), lax.axis_index("resp")
        self.s, self.r = s, r
        self.at = {"y": s // SIDE, "z": s % SIDE, "x": r // 2, "core": r % 2}

    def step(self, axis, by):
        c = dict(self.at)
        c[axis] = (c[axis] + by + SIDE) % SIDE if axis != "core" else 1 - c[axis]
        return (c["y"] * SIDE + c["z"], c["x"] * 2 + c["core"])

    def index(self, axis, by=0):
        return (self.at[axis] + by + SIDE) % SIDE


AXES = (("z", "y"), ("y", "z"))
BACK, AHEAD = 0, 1


def remote(src, dst, send, recv, to):
    return pltpu.make_async_remote_copy(
        src_ref=src, dst_ref=dst, send_sem=send, recv_sem=recv, device_id=to, device_id_type=MESH
    )


def gather(here, mine, full, near_send, near_recv, far_send, far_recv):
    started = []
    orders = (0, -1, 1, 2)

    def go(copy):
        copy.start()
        started.append(copy)

    def near(X, src, dst, way, kind):
        to = here.step(AXES[X][0], 1 if way == BACK else -1)
        return remote(src, dst, near_send.at[X, way, kind], near_recv.at[X, way, kind], to)

    def far(X, src, dst, way, kind):
        to = here.step(AXES[X][1], 1 if way == BACK else -1)
        return remote(src, dst, far_send.at[X, way, kind], far_recv.at[X, way, kind], to)

    def slot(X, by2, by1):
        first, second = AXES[X]
        return full[X].at[here.index(second, by2), here.index(first, by1)]

    def along(X, k):
        ref = mine[X] if k == 0 else slot(X, 0, orders[k])
        for way in (BACK, AHEAD):
            go(far(X, ref, slot(X, 0, orders[k]), way, k))

    def landed(k):
        for X in (0, 1):
            for way in (BACK, AHEAD):
                ref = slot(X, -1 if way == BACK else 1, orders[k])
                far(X, ref, ref, way, k).wait_recv()
                if way == (BACK if k < 2 else AHEAD):
                    go(far(X, ref, ref, way, 4 + k))

    top, low = pl.ds(0, UNIT), pl.ds(UNIT, UNIT)
    for X in (0, 1):
        for way in (BACK, AHEAD):
            go(near(X, mine[X], slot(X, 0, 0), way, 0))
    for X in (0, 1):
        along(X, 0)
    yield "sent"
    for way, by, part in ((BACK, -1, top), (AHEAD, 1, low)):
        for X in (0, 1):
            ref = slot(X, 0, by)
            near(X, ref, ref, way, 0).wait_recv()
            go(near(X, ref.at[part], ref.at[part], way, 1))
            along(X, 1 if way == BACK else 2)
    yield "near"
    landed(0)
    yield "far0"
    for X in (0, 1):
        ref = slot(X, 0, 2)
        near(X, ref.at[top], ref.at[top], BACK, 1).wait_recv()
        near(X, ref.at[low], ref.at[low], AHEAD, 1).wait_recv()
        along(X, 3)
    yield "line"
    for k in (1, 2, 3):
        landed(k)
        yield "far" + str(k)
    for k in (0, 1, 2, 3):
        for X in (0, 1):
            ref = slot(X, 2, orders[k])
            far(X, ref, ref, BACK if k < 2 else AHEAD, 4 + k).wait_recv()
        yield "past" + str(k)
    for copy in started:
        copy.wait_send()


def greet(devices, count):
    barrier = pltpu.get_barrier_semaphore()
    for d in devices:
        pl.semaphore_signal(barrier, inc=1, device_id=d, device_id_type=MESH)
    pl.semaphore_wait(barrier, count)


def heads_first(ref, base, rows, heads):
    return jnp.concatenate([ref[pl.ds(base, rows), h * HD : (h + 1) * HD] for h in range(heads)], axis=0)


def transpose_values(v):
    return jnp.transpose(v.astype(F32)).astype(BF16)


def spread_kernel(
    lengths, groups, q, keys, values,
    full0, full1, everyone, own_o, own_st,
    qbuf, kbuf, vbuf, lens, marks, scores, vt, tile,
    near_send, near_recv, far_send, far_recv, group_send, group_recv, load,
):
    here = Place()
    s, r = here.s, here.r
    n, hist, _ = keys.shape
    C = q.shape[0] // n
    H = q.shape[1] // HD
    rows = C * H
    seqs = SIDE * SIDE
    loads = [
        pltpu.make_async_copy(src, dst, load.at[i])
        for i, (src, dst) in enumerate(((groups, marks), (lengths, lens), (q, qbuf), (keys, kbuf), (values, vbuf)))
    ]
    for copy in loads:
        copy.start()
    others = [((s + d) % seqs, r) for d in range(1, seqs)]
    greet(others, seqs - 1)
    mine = [q.at[:, X * HALF : (X + 1) * HALF] for X in (0, 1)]
    full = (full0, full1)
    steps = gather(here, mine, full, near_send, near_recv, far_send, far_recv)
    next(steps)
    loads[0].wait()
    lane = lax.broadcasted_iota(jnp.int32, tile.shape, 1)
    mark = jnp.zeros(tile.shape, jnp.int32)
    for i in range(n):
        mark = jnp.where(lane == i, marks[i], mark)
    tile[...] = mark
    told = []
    for d, to in enumerate(others):
        copy = remote(tile, everyone.at[s], group_send.at[d], group_recv.at[d], to)
        copy.start()
        told.append(copy)
    for copy in loads[1:]:
        copy.wait()
    for X in (0, 1):
        first, second = AXES[X]
        full[X][here.index(second), here.index(first)] = qbuf[:, X * HALF : (X + 1) * HALF]
    everyone[s] = mark
    own_st[...] = jnp.full(own_st.shape, NEG, F32)
    vt[HD:, :] = jnp.ones((ONES, hist), BF16)

    def own(u, _):
        base = pl.multiple_of(u * C, C)
        qa = heads_first(qbuf, base, C, H)
        sc = lax.dot_general(kbuf[u], qa, (((1,), (1,)), ((), ())), preferred_element_type=F32)
        pos = lax.broadcasted_iota(jnp.int32, (hist, rows), 0)
        upto = lens[u] + lax.broadcasted_iota(jnp.int32, (1, rows), 1) % C
        sc = jnp.where(pos <= upto, sc, NEG)
        scores[...] = sc
        for j in range(0, hist, HD):
            vt[:HD, j : j + HD] = transpose_values(vbuf[u, j : j + HD, :])
        shift = jnp.max(sc, axis=0, keepdims=True) * C2
        p = jnp.exp2(scores[...] * C2 - shift).astype(BF16)
        out = jnp.dot(vt[...], p, preferred_element_type=F32)
        total = out[HD : HD + 1, :]
        lse = shift + jnp.log2(total)
        out = out[:HD, :] * (1.0 / total)
        for X in (0, 1):
            own_st[X, u // 2, pl.ds(u % 2, 1), :] = lse[:, X * HD : (X + 1) * HD]
            t = jnp.transpose(out[:, X * HD : (X + 1) * HD])
            for w in range(HD // C):
                own_o[X, u // 2, pl.ds(pl.multiple_of(u % 2 * C, C), C), w * HD : (w + 1) * HD] = t[w * C : (w + 1) * C, :]
        return 0

    lax.fori_loop(0, n // 2, own, 0)
    for stage in steps:
        if stage == "far0":
            lax.fori_loop(n // 2, n, own, 0)
    for d, copy in enumerate(told):
        copy.wait_send()
        src = everyone.at[(s + seqs - 1 - d) % seqs]
        remote(src, src, group_send.at[d], group_recv.at[d], others[d]).wait_recv()


def spread(lengths, groups, q, keys, values):
    n, hist, _ = keys.shape
    C = q.shape[0] // n
    rows = C * q.shape[1] // HD
    vm, hbm = (pl.BlockSpec(memory_space=m) for m in (pltpu.VMEM, pltpu.HBM))
    dma = pltpu.SemaphoreType.DMA
    full = jax.ShapeDtypeStruct((SIDE, SIDE, n * C, HALF), BF16)
    return pl.pallas_call(
        spread_kernel,
        out_shape=(
            full,
            full,
            jax.ShapeDtypeStruct((SIDE * SIDE, 8, HD), jnp.int32),
            jax.ShapeDtypeStruct((2, 2, UNIT, HALF), F32),
            jax.ShapeDtypeStruct((2, 2, 8, HD), F32),
        ),
        in_specs=[hbm] * 5,
        out_specs=(vm,) * 5,
        scratch_shapes=[
            pltpu.VMEM(q.shape, BF16),
            pltpu.VMEM(keys.shape, BF16),
            pltpu.VMEM(keys.shape, BF16),
            pltpu.SMEM((n,), jnp.int32),
            pltpu.SMEM((n,), jnp.int32),
            pltpu.VMEM((hist, rows), F32),
            pltpu.VMEM((HD + ONES, hist), BF16),
            pltpu.VMEM((8, HD), jnp.int32),
            dma((2, 2, 2)), dma((2, 2, 2)), dma((2, 2, 8)), dma((2, 2, 8)),
            dma((SIDE * SIDE - 1,)), dma((SIDE * SIDE - 1,)), dma((5,)),
        ],
        compiler_params=pltpu.CompilerParams(collective_id=1, has_side_effects=True, vmem_limit_bytes=24 << 20),
        name="spread_queries",
    )(*(pltpu.with_memory_space_constraint(a, pltpu.HBM) for a in (lengths, groups, q, keys, values)))


def prompt_kernel(sizes, everyone, seg, q0, q1, k, v, o0, o1, st0, st1, lists, count, sa, sb, vt, ka, groups, load):
    fetch = pltpu.make_async_copy(everyone.at[:, 0:1], groups, load)
    fetch.start()
    n_resp = everyone.shape[0] * 4
    C = q0.shape[0] // n_resp
    H = 2 * HALF // HD
    L = k.shape[0]
    rows = C * H
    per = 4
    for ref in (st0, st1):
        ref[...] = jnp.full(ref.shape, NEG, F32)
    for ref in (o0, o1):
        ref[...] = jnp.zeros(ref.shape, BF16)
    for j in range(0, L, HD):
        vt[:HD, j : j + HD] = transpose_values(v[j : j + HD, :])
    vt[HD:, :] = jnp.ones((ONES, L), BF16)
    sg = seg[...]
    cut = [jnp.int32(0)] + [jnp.sum((sg < g).astype(jnp.int32)) for g in range(1, G)] + [jnp.int32(L)]
    lane = lax.broadcasted_iota(jnp.int32, (1, HD), 1)
    low, high = jnp.zeros((1, HD), jnp.int32), jnp.full((1, HD), L, jnp.int32)
    for g in range(G):
        low = jnp.where(lane == g, cut[g], low)
        high = jnp.where(lane == g, cut[g + 1], high)
        count[g] = 0
    ka[:, :HD] = k[...]
    pos = lax.broadcasted_iota(jnp.int32, (L, HD), 0)
    ka[:, HD:] = jnp.where(jnp.logical_and(pos >= low, pos < high), 0.0, NEG).astype(BF16)

    def scan(r, _):
        g = groups[r // per, 0, r % per]
        c = count[g]
        lists[g * n_resp + c] = r
        count[g] = c + 1
        return 0

    fetch.wait()
    lax.fori_loop(0, n_resp, scan, 0)

    def spots(r):
        s, u = r // per, r % per
        turned = (s % SIDE) * SIDE + s // SIDE
        return s, turned, u

    def score(g, n, i, p0, T, M, dst):
        tops = []
        for m in range(M):
            s, turned, u = spots(lists[g * n_resp + jnp.minimum(M * i + m, n - 1)])
            base0 = pl.multiple_of((s * per + u) * C, C)
            base1 = pl.multiple_of((turned * per + u) * C, C)
            mine = jnp.concatenate([heads_first(q0, base0, C, H // 2), heads_first(q1, base1, C, H // 2)], axis=0)
            flag = (lax.broadcasted_iota(jnp.int32, (rows, HD), 1) == g).astype(F32).astype(BF16)
            qa = jnp.concatenate([mine, flag], axis=1)
            sc = lax.dot_general(ka[pl.ds(p0, T), :], qa, (((1,), (1,)), ((), ())), preferred_element_type=F32)
            dst[:T, m * rows : (m + 1) * rows] = sc
            tops.append(jnp.max(sc, axis=0, keepdims=True))
        return tuple(tops)

    def soft(g, n, i, p0, T, M, src, tops):
        for m in range(M):
            s, turned, u = spots(lists[g * n_resp + jnp.minimum(M * i + m, n - 1)])
            shift = tops[m] * C2
            p = jnp.exp2(src[:T, m * rows : (m + 1) * rows] * C2 - shift).astype(BF16)
            out = jnp.dot(vt[:, pl.ds(p0, T)], p, preferred_element_type=F32)
            total = out[HD : HD + 1, :]
            lse = shift + jnp.log2(total)
            out = out[:HD, :] * (1.0 / total)
            for X, o, st, place in ((0, o0, st0, turned), (1, o1, st1, s)):
                st[pl.ds((place * 2 + u // 2) * 8 + u % 2, 1), :] = lse[:, X * HD : (X + 1) * HD]
                base = pl.multiple_of((place * per + u) * C, C)
                t = jnp.transpose(out[:, X * HD : (X + 1) * HD]).astype(BF16)
                for w in range(HD // C):
                    o[pl.ds(base, C), w * HD : (w + 1) * HD] = t[w * C : (w + 1) * C, :]

    for g in range(G):
        lo, hi, n = cut[g], cut[g + 1], count[g]
        start = lo // HD * HD
        for T, less in zip(sizes, (0,) + sizes[:-1]):
            p0 = pl.multiple_of(jnp.minimum(start, L - T), HD)
            fits = hi - p0 <= T
            if less:
                fits = jnp.logical_and(fits, hi - jnp.minimum(start, L - less) > less)

            @pl.when(jnp.logical_and(jnp.logical_and(hi > lo, n > 0), fits))
            def _(T=T, p0=p0, n=n, g=g):
                M = 1 if T == L else 2
                turns = (n + M - 1) // M

                def two(i, tops):
                    j = 2 * i
                    after = score(g, n, j + 1, p0, T, M, sb)
                    soft(g, n, j, p0, T, M, sa, tops)
                    then = score(g, n, j + 2, p0, T, M, sa)
                    soft(g, n, j + 1, p0, T, M, sb, after)
                    return then

                lax.fori_loop(0, (turns + 1) // 2, two, score(g, n, 0, p0, T, M, sa))


def prompt_part(everyone, seg, q0, q1, k, v):
    L = k.shape[0]
    rows, width = q0.shape
    n_resp = everyone.shape[0] * 4
    R = rows // n_resp * 2 * width // HD
    vm = pl.BlockSpec(memory_space=pltpu.VMEM)
    part = jax.ShapeDtypeStruct(q0.shape, BF16)
    stat = jax.ShapeDtypeStruct((rows // UNIT * 8, HD), F32)
    sizes = tuple(L * i // 4 for i in (1, 2, 3, 4))
    return pl.pallas_call(
        functools.partial(prompt_kernel, sizes),
        out_shape=(part, part, stat, stat),
        in_specs=[vm] * 6,
        out_specs=(vm,) * 4,
        scratch_shapes=[
            pltpu.SMEM((G * n_resp,), jnp.int32),
            pltpu.SMEM((G,), jnp.int32),
            pltpu.VMEM((L, 2 * R), F32),
            pltpu.VMEM((L, 2 * R), F32),
            pltpu.VMEM((HD + ONES, L), BF16),
            pltpu.VMEM((L, 2 * HD), BF16),
            pltpu.SMEM((everyone.shape[0], 1, HD), jnp.int32),
            pltpu.SemaphoreType.DMA,
        ],
        compiler_params=pltpu.CompilerParams(vmem_limit_bytes=20 << 20),
        name="prompt_part",
    )(everyone, seg.reshape(-1, HD), q0, q1, k, v)


def merge(parts):
    top = functools.reduce(jnp.maximum, [st for _, st in parts])
    weights = [jnp.exp2(st - top) for _, st in parts]
    total = functools.reduce(jnp.add, weights)
    scale = 1.0 / total
    turned = [jnp.transpose(w * scale) for w in weights]
    C = UNIT // 2
    lines = []
    for u in range(2):
        line = []
        for h in range(HALF // HD):
            acc = None
            for (o, _), t in zip(parts, turned):
                term = o[u * C : (u + 1) * C, h * HD : (h + 1) * HD].astype(F32) * t[h * C : (h + 1) * C, u : u + 1]
                acc = term if acc is None else acc + term
            line.append(acc)
        lines.append(jnp.concatenate(line, axis=1))
    return jnp.concatenate(lines, axis=0).astype(BF16), top + jnp.log2(total)


class Ring:
    def __init__(self, here, axis, spot, src, in2, in1, out, sems):
        self.here, self.axis, self.spot, self.src, self.in2, self.in1, self.out = here, axis, spot, src, in2, in1, out
        self.send, self.recv = sems
        self.pieces, self.units = in2[0].shape[1], in2[0].shape[2]
        self.started = []

    def copy(self, src, dst, way, kind, p):
        to = self.here.step(self.axis, 1 if way == BACK else -1)
        return [
            remote(a, b, self.send.at[way, kind, p, i], self.recv.at[way, kind, p, i], to)
            for i, (a, b) in enumerate(zip(src, dst))
        ]

    def go(self, copies):
        for c in copies:
            c.start()
            self.started.append(c)

    def line(self, by, group, p):
        return [ref.at[self.here.index(self.axis, by), self.spot(group, p)] for ref in self.src]

    def got(self, way, group, p):
        return [ref.at[way, group * self.pieces + p] for ref in self.in1]

    def begin_far(self, p):
        for way in (BACK, AHEAD):
            self.go(self.copy(self.line(2, way, p), [ref.at[way, p] for ref in self.in2], way, 0, p))

    def begin_near(self, way, p):
        by = 1 if way == BACK else -1
        self.go(self.copy(self.line(by, 1 - way, p), self.got(way, 1 - way, p), way, 1, p))

    def pass_on(self, way, p):
        landed = [ref.at[way, p] for ref in self.in2]
        for c in self.copy(landed, landed, way, 0, p):
            c.wait_recv()
        i, spot = self.here.index(self.axis, 1 if way == BACK else -1), self.spot(way, p)
        for u in range(self.units):
            mine = [ref[i, spot, u] for ref in self.src]
            theirs = [ref[way, p, u] for ref in self.in2]
            for ref, value in zip(self.out, merge([mine, theirs])):
                ref[way, p, u] = value
        self.go(self.copy([ref.at[way, p] for ref in self.out], self.got(way, way, p), way, 2, p))

    def arrive(self, group, p):
        for way in (BACK, AHEAD):
            refs = self.got(way, group, p)
            for c in self.copy(refs, refs, way, 2 if way == group else 1, p):
                c.wait_recv()

    def total(self, group, p, u, extra=()):
        i, spot = self.here.index(self.axis), self.spot(group, p)
        parts = [[ref[i, spot, u] for ref in self.src]]
        parts += [[ref[way, group * self.pieces + p, u] for ref in self.in1] for way in (BACK, AHEAD)]
        return merge(parts + list(extra))

    def finish(self):
        for c in self.started:
            c.wait_send()


ROUNDS = (
    ((0, 0), (0, -1), (0, 1), (-1, 0)),
    ((1, 0), (-1, -1), (1, -1), (-1, 1)),
    ((1, 1), (0, 2), (2, 0), (-1, 2)),
    ((1, 2), (2, -1), (2, 1), (2, 2)),
)


def choose(index, values):
    out = jnp.int32(values[0])
    for i in range(1, len(values)):
        out = jnp.where(index == i, values[i], out)
    return out


def project_kernel(
    o0, o1, st0, st1, own_o, own_st, weight, result,
    a_in2, a_in2s, a_in1, a_in1s, a_out, a_outs, a_sum, a_sums,
    b_in2, b_in2s, b_in1, b_in1s, b_out, b_outs,
    att, full0, full1, part, swapped, sums, x_in, final, moved,
    a_send, a_recv, b_send, b_recv, x_send, x_recv,
    near_send, near_recv, far_send, far_recv, core_send, core_recv, move_send, move_recv, last_send, last_recv, local,
):
    here = Place()
    s, r = here.s, here.r
    x, core = here.at["x"], here.at["core"]
    mate = here.step("core", 1)
    steps_to = [[choose(x, [o[k] for o in owners]) for k in (0, 1)] for owners in ROUNDS]

    def beside(i, sign):
        dy, dz = steps_to[i]
        return here.index("y", sign * dy), here.index("z", sign * dz)

    still = x == 0

    def moves(i, act):
        if i == 0:
            pl.when(jnp.logical_not(still))(act)
        else:
            act()

    row = [(s, (r + d) % (2 * SIDE)) for d in range(1, 2 * SIDE)]
    barrier = pltpu.get_barrier_semaphore()
    for d in [here.step(axis, by) for axis in ("y", "z") for by in (1, -1)] + row:
        pl.semaphore_signal(barrier, inc=1, device_id=d, device_id_type=MESH)
    for i in range(len(ROUNDS)):
        y, z = beside(i, -1)
        moves(i, lambda: pl.semaphore_signal(barrier, inc=1, device_id=(y * SIDE + z, r), device_id_type=MESH))
    pl.semaphore_wait(barrier, 4 + len(row) + len(ROUNDS) - still.astype(jnp.int32))

    o, st = (o0, o1), (st0, st1)
    one, two = [], []
    order = ((2, 0), (1, -1))
    for X in (0, 1):
        spot = lambda way, p, X=X: here.index(AXES[X][1], order[way][p])
        one.append(
            Ring(
                here, AXES[X][0], spot, (o[X], st[X]), (a_in2.at[X], a_in2s.at[X]), (a_in1.at[X], a_in1s.at[X]),
                (a_out.at[X], a_outs.at[X]), (a_send.at[X], a_recv.at[X]),
            )
        )
        two.append(
            Ring(
                here, AXES[X][1], lambda way, p: way, (a_sum.at[X], a_sums.at[X]), (b_in2.at[X], b_in2s.at[X]),
                (b_in1.at[X], b_in1s.at[X]), (b_out.at[X], b_outs.at[X]), (b_send.at[X], b_recv.at[X]),
            )
        )

    def settle(group, p):
        for X in (0, 1):
            one[X].arrive(group, p)
            d = one[X].spot(group, p)
            for u in range(2):
                value, stat = one[X].total(group, p, u)
                a_sum[X, d, u, 0] = value
                a_sums[X, d, u, 0] = stat

    both = (0, 1)
    for p in range(2):
        for X in both:
            one[X].begin_far(p)
    for p in range(2):
        for X in both:
            for way in (BACK, AHEAD):
                one[X].begin_near(way, p)
        for way in (BACK, AHEAD):
            for X in both:
                one[X].pass_on(way, p)
    settle(BACK, 0)
    for X in both:
        two[X].begin_far(0)
    settle(AHEAD, 0)
    for X in both:
        two[X].begin_near(BACK, 0)
    settle(AHEAD, 1)
    for X in both:
        two[X].begin_near(AHEAD, 0)
    for way in (BACK, AHEAD):
        for X in both:
            two[X].pass_on(way, 0)
    settle(BACK, 1)
    for X in both:
        for way in (BACK, AHEAD):
            two[X].arrive(way, 0)
            value, _ = two[X].total(way, 0, 0, [(own_o[X, way], own_st[X, way])])
            att[X, way * UNIT : (way + 1) * UNIT, :] = value

    full = (full0, full1)
    steps = gather(here, (att.at[0], att.at[1]), full, near_send, near_recv, far_send, far_recv)
    next(steps)
    for X in (0, 1):
        first, second = AXES[X]
        full[X][here.index(second), here.index(first)] = att[X]

    crossing = {}

    def terms(i):
        for j, (dy, dz) in enumerate(ROUNDS[i]):
            y, z = here.index("y", dy), here.index("z", dz)
            value = jnp.dot(full0[y, z], weight[:HALF, :], preferred_element_type=F32)
            value += jnp.dot(full1[z, y], weight[HALF:, :], preferred_element_type=F32)
            value = value.astype(BF16)
            for c in range(2):
                part[i, c, j] = value[c * UNIT : (c + 1) * UNIT]
        crossing[i] = remote(part.at[i, 1 - core], swapped.at[i], core_send.at[i], core_recv.at[i], mate)
        crossing[i].start()

    def shift(i, d):
        j = here.index("x", d)
        return remote(sums.at[i, j], x_in.at[i, d - 1], x_send.at[i, d - 1], x_recv.at[i, d - 1], here.step("x", d))

    def cross(i):
        crossing[i].wait_recv()
        for d in (2, 1, 3, 0):
            j = here.index("x", d)
            sums[i, j] = (part[i, core, j].astype(F32) + swapped[i, j].astype(F32)).astype(BF16)
            if d:
                shift(i, d).start()

    def move(i):
        y, z = beside(i, 1)
        return remote(final.at[i], moved.at[i], move_send.at[i], move_recv.at[i], (y * SIDE + z, r))

    def deliver(i):
        for d in (1, 2, 3):
            shift(i, d).wait_recv()
        value = sums[i, x].astype(F32)
        for d in (1, 2, 3):
            value += x_in[i, d - 1].astype(F32)
        value = value.astype(BF16)
        final[i] = value
        moves(i, lambda: move(i).start())
        if i == 0:

            @pl.when(still)
            def _():
                moved[i] = value

    def last(i):
        y, z = beside(i, -1)
        owner = y * 2 + z // 2
        dst = result.at[
            pl.ds(pl.multiple_of(core * UNIT, UNIT), UNIT), pl.ds(pl.multiple_of(z % 2 * HALF, HALF), HALF)
        ]
        away = remote(moved.at[i], dst, last_send.at[i], last_recv.at[z % 2, core], (s, owner))
        return away, pltpu.make_async_copy(moved.at[i], dst, local.at[i]), owner == r

    def forward(i):
        moves(i, lambda: move(i).wait_recv())
        away, home, stays = last(i)
        pl.when(jnp.logical_not(stays))(away.start)
        pl.when(stays)(home.start)

    plan = {
        "far0": (terms, 0), "far1": (cross, 0), "far2": (terms, 1, deliver, 0), "far3": (cross, 1, forward, 0),
        "past1": (terms, 2, deliver, 1), "past2": (cross, 2, forward, 1),
        "past3": (terms, 3, deliver, 2, cross, 3, forward, 2),
    }
    for stage in steps:
        todo = plan.get(stage, ())
        for k in range(0, len(todo), 2):
            todo[k](todo[k + 1])
    deliver(3)
    forward(3)

    for ring in one + two:
        ring.finish()
    for i in range(len(ROUNDS)):
        crossing[i].wait_send()
        for d in (1, 2, 3):
            shift(i, d).wait_send()
        moves(i, lambda: move(i).wait_send())
        away, home, stays = last(i)
        pl.when(jnp.logical_not(stays))(away.wait_send)
        pl.when(stays)(home.wait)
    spots = {(dy % SIDE) * SIDE + dz % SIDE: j for owners in ROUNDS for j, (dy, dz) in enumerate(owners)}
    for j in range(2):
        sender = 2 * r + j
        dy, dz = here.index("y", -(sender // SIDE)), here.index("z", -(sender % SIDE))
        column = choose(dy * SIDE + dz, [spots[i] for i in range(SIDE * SIDE)])
        for c in range(2):
            dst = result.at[c * UNIT : (c + 1) * UNIT, j * HALF : (j + 1) * HALF]
            copy = remote(dst, dst, last_send.at[0], last_recv.at[j, c], mate)
            pl.when(jnp.logical_not(jnp.logical_and(column == x, core == c)))(copy.wait_recv)


def project(o0, o1, st0, st1, own_o, own_st, weight):
    vm = pl.BlockSpec(memory_space=pltpu.VMEM)
    dma = pltpu.SemaphoreType.DMA
    block, stat = (UNIT, HALF), (8, HD)
    rows = 2 * UNIT
    rounds = len(ROUNDS)
    o0, o1 = (a.reshape(SIDE, SIDE, 2, *block) for a in (o0, o1))
    st0, st1 = (a.reshape(SIDE, SIDE, 2, *stat) for a in (st0, st1))
    pair = lambda *lead: [pltpu.VMEM(lead + block, BF16), pltpu.VMEM(lead + stat, F32)]
    return pl.pallas_call(
        project_kernel,
        out_shape=jax.ShapeDtypeStruct((rows, 2 * HALF), BF16),
        in_specs=[vm] * 7,
        out_specs=vm,
        scratch_shapes=[
            *pair(2, 2, 2, 2), *pair(2, 2, 4, 2), *pair(2, 2, 2, 2), *pair(2, SIDE, 2, 1),
            *pair(2, 2, 1, 1), *pair(2, 2, 2, 1), *pair(2, 2, 1, 1),
            pltpu.VMEM((2, rows, HALF), BF16),
            pltpu.VMEM((SIDE, SIDE, rows, HALF), BF16),
            pltpu.VMEM((SIDE, SIDE, rows, HALF), BF16),
            pltpu.VMEM((rounds, 2, SIDE) + block, BF16),
            pltpu.VMEM((rounds, SIDE) + block, BF16),
            pltpu.VMEM((rounds, SIDE) + block, BF16),
            pltpu.VMEM((rounds, SIDE - 1) + block, BF16),
            pltpu.VMEM((rounds,) + block, BF16),
            pltpu.VMEM((rounds,) + block, BF16),
            dma((2, 2, 3, 2, 2)), dma((2, 2, 3, 2, 2)), dma((2, 2, 3, 1, 2)), dma((2, 2, 3, 1, 2)),
            dma((rounds, SIDE - 1)), dma((rounds, SIDE - 1)),
            dma((2, 2, 2)), dma((2, 2, 2)), dma((2, 2, 8)), dma((2, 2, 8)),
            dma((rounds,)), dma((rounds,)), dma((rounds,)), dma((rounds,)), dma((rounds,)), dma((2, 2)), dma((rounds,)),
        ],
        compiler_params=pltpu.CompilerParams(collective_id=2, has_side_effects=True, vmem_limit_bytes=34 << 20),
        name="merge_and_project",
    )(o0, o1, st0, st1, own_o, own_st, weight)


def per_device(
    queries, prompt_keys, prompt_values, prompt_segment, own_keys, own_values, resp_lengths, resp_groups, out_weight
):
    n, C, width = queries.shape
    q = queries.reshape(n * C, width)
    full0, full1, everyone, own_o, own_st = spread(resp_lengths, resp_groups, q, own_keys, own_values)
    flat = lambda a: a.reshape(-1, HALF)
    parts = prompt_part(everyone, prompt_segment, flat(full0), flat(full1), prompt_keys, prompt_values)
    return project(*parts, own_o, own_st, out_weight).reshape(n, C, width)


def solution(mesh):
    in_specs = (
        P("seq", None, "resp"),
        P("seq", "resp"),
        P("seq", "resp"),
        P("seq"),
        P("seq", None, "resp"),
        P("seq", None, "resp"),
        P("seq"),
        P("seq"),
        P("resp", "seq"),
    )
    return jax.shard_map(
        per_device, mesh=mesh, in_specs=in_specs, out_specs=P("seq", None, "resp"), check_vma=False
    )
```
